32 devices in a mesh: row: 4 (over y, core), col: 8 (over z, x).
Axes of the slice: x: 2, y: 2, z: 4, core: 2. Of those that a mesh axis runs over, the one named last changes fastest.
Arguments:
- features: bfloat16 [8192, 128], P(('col', 'row')), may hold values from -6 to 6
- weight: bfloat16 [128, 128], replicated, may hold values from -0.5 to 0.5
- tiles: bfloat16 [4, 8, 44, 128, 128], P('row', 'col'), may hold values from -0.15625 to 0.15625
- tile_slots: int32 [4, 8, 44], P('row', 'col'), may hold values from 0 to 127, as said below
- tile_counts: int32 [4, 8], P('row', 'col'), may hold values from 5 to 44, as said below
- cotangent: bfloat16 [8192, 128], P(('row', 'col')), may hold values from -6 to 6
Outputs:
- hidden: bfloat16 [8192, 128], P(('row', 'col'))
- feature_grad: bfloat16 [8192, 128], P(('col', 'row'))
- weight_grad: float32 [128, 128], replicated
The draws below stay inside these ranges and needn't reach their ends.
Inputs may be any that keep to these rules, and one draw needn't show every extreme that they name: `tile_slots`: the slots of one block are distinct. `tile_counts`: some block has all 44 slots live.
All inputs are finite; a program needn't handle non-finite values.
Results may differ from the reference program's by a relative error of at most 0.006.
Values may be sent and summed in bfloat16 or wider, within the bound.
No kernel may reach another device: no remote copies, remote signals or barrier semaphores. Data moves between devices by JAX's collectives and lax.ppermute only.
A program may use at most 128 MiB of HBM per device.

```python
import math
import jax
import jax.numpy as jnp
from jax import lax

FEAT = 128
TILE = 128
SHARE = 256
TROWS = 16
MAXT = 44
NODES = 8192
N_ROW = 4
N_COL = 8


def draw_tile_slots(key, part):
    tile_rows = SHARE * N_COL // TILE
    tile_cols = SHARE * N_ROW // TILE
    keys = jax.random.split(jax.random.fold_in(key, 11), N_ROW * N_COL)
    picked = jax.vmap(lambda sub: jax.random.permutation(sub, tile_rows * tile_cols)[:MAXT])(keys)
    return picked.astype(jnp.int32).reshape(N_ROW, N_COL, MAXT)


def draw_tile_counts(key, part):
    blocks = N_ROW * N_COL
    lowest = MAXT // 8
    raw = jax.random.randint(jax.random.fold_in(key, 21), (blocks,), 0, 64)
    counts = lowest + raw * raw * (MAXT - lowest) // (63 * 63)
    fullest = jax.random.randint(jax.random.fold_in(key, 22), (), 0, blocks)
    places = jnp.arange(blocks, dtype=jnp.int32)
    counts = jnp.where(places == fullest, MAXT, counts)
    counts = jnp.where(places == (fullest + 1) % blocks, lowest, counts)
    return counts.astype(jnp.int32).reshape(N_ROW, N_COL)


def steps_of(stream_key, shape, shards, least, largest):
    level = 1.0
    for axis_at, shards_of in shards:
        steps = jax.random.uniform(jax.random.fold_in(jax.random.fold_in(stream_key, 6), axis_at), (shards_of,), jnp.float32, least / len(shards), largest / len(shards))
        level = level * jnp.repeat(jnp.exp(steps), shape[axis_at] // shards_of).reshape((-1,) + (1,) * (len(shape) - 1 - axis_at))
    return level


def gaussian(own_key, extent, width, limit, cuts=(), kind=jnp.bfloat16):
    gain = steps_of(own_key, extent, cuts, -0.22, 0.18) if cuts else 1.0
    drawn = jax.random.normal(own_key, extent, jnp.float32) * width * gain
    return jnp.minimum(jnp.maximum(drawn, -limit), limit).astype(kind)


def setup_inputs(seed: int = 0) -> dict:
    splits = jax.random.split(jax.random.key(seed), 7)
    return {
        "features": gaussian(splits[0], (NODES, FEAT), 1.0, 6.0, ((0, 32),)),
        "weight": gaussian(splits[1], (FEAT, FEAT), FEAT ** -0.5, 0.5),
        "tiles": gaussian(splits[2], (N_ROW, N_COL, MAXT, TILE, TILE), (TILE * MAXT * N_COL // (2 * TROWS)) ** -0.5, 0.15625, ((0, 4), (1, 8))),
        "tile_slots": draw_tile_slots(jax.random.fold_in(splits[6], 71), 0),
        "tile_counts": draw_tile_counts(jax.random.fold_in(splits[6], 71), 0),
        "cotangent": gaussian(splits[5], (NODES, FEAT), 1.0, 6.0, ((0, 32),)),
    }


def silu_grad(values):
    sig = jax.nn.sigmoid(values)
    return sig * (1.0 + values * (1.0 - sig))

def reference(features, weight, tiles, tile_slots, tile_counts, cotangent):
    tile_rows = SHARE * N_COL // TILE
    tile_cols = SHARE * N_ROW // TILE
    block_rows = SHARE * N_COL
    block_cols = SHARE * N_ROW
    projected = jnp.dot(features, weight, preferred_element_type=jnp.float32).astype(jnp.bfloat16)
    proj_blocks = projected.reshape(N_COL, block_cols, FEAT)
    live_mask = (jnp.arange(MAXT, dtype=jnp.int32)[None, None, :] < tile_counts[:, :, None]).astype(jnp.float32)

    def fwd_one(tile_vals, slot_ids, mask_row, proj_block):
        gathered = proj_block.reshape(tile_cols, TILE, FEAT)[slot_ids % tile_cols]
        products = jnp.einsum('tij,tjf->tif', tile_vals.astype(jnp.float32), gathered.astype(jnp.float32)) * mask_row[:, None, None]
        return jax.ops.segment_sum(products, slot_ids // tile_cols, tile_rows).reshape(block_rows, FEAT)

    def fwd_row(inputs):
        tile_vals, slot_ids, mask_rows = inputs
        return lax.optimization_barrier(jnp.sum(jax.vmap(fwd_one)(tile_vals, slot_ids, mask_rows, proj_blocks), axis=0))
    summed = lax.map(fwd_row, (tiles, tile_slots, live_mask)).reshape(NODES, FEAT)
    hidden = jax.nn.silu(summed).astype(jnp.bfloat16)
    grad_sum = (cotangent.astype(jnp.float32) * silu_grad(summed)).astype(jnp.bfloat16)
    grad_rows = grad_sum.reshape(N_ROW, block_rows, FEAT)

    def bwd_one(tile_vals, slot_ids, mask_row, grad_block):
        gathered = grad_block.reshape(tile_rows, TILE, FEAT)[slot_ids // tile_cols]
        products = jnp.einsum('tji,tjf->tif', tile_vals.astype(jnp.float32), gathered.astype(jnp.float32)) * mask_row[:, None, None]
        return jax.ops.segment_sum(products, slot_ids % tile_cols, tile_cols).reshape(block_cols, FEAT)

    def bwd_step(accum, inputs):
        tile_vals, slot_ids, mask_rows, grad_block = inputs
        terms = jax.vmap(bwd_one, in_axes=(0, 0, 0, None))(tile_vals, slot_ids, mask_rows, grad_block)
        return (accum + terms, None)
    start = jnp.zeros((N_COL, block_cols, FEAT), jnp.float32)
    accum, _ = lax.scan(bwd_step, start, (tiles, tile_slots, live_mask, grad_rows))
    grad_proj = accum.reshape(NODES, FEAT).astype(jnp.bfloat16)
    feature_grad = jnp.dot(grad_proj, weight.T, preferred_element_type=jnp.float32).astype(jnp.bfloat16)
    weight_grad = jnp.dot(features.T, grad_proj, preferred_element_type=jnp.float32) / math.sqrt(NODES)
    return (hidden, feature_grad, weight_grad)
```

```python
import functools
import math

import jax
import jax.numpy as jnp
from jax import lax
from jax.experimental import pallas as pl
from jax.experimental.pallas import tpu as pltpu
from jax.sharding import PartitionSpec as P

F32 = jnp.float32
BF16 = jnp.bfloat16
VMEM_LIMIT = 24 * 1024 * 1024
DENSE_LIMIT = 12 * 1024 * 1024


def in_vmem(x):
    return pltpu.with_memory_space_constraint(x, pltpu.VMEM)


def in_hbm(x):
    return pltpu.with_memory_space_constraint(x, pltpu.HBM)


def kernel_call(kernel, outs, flops, name, in_specs, scratch=(), limit=VMEM_LIMIT):
    shapes = [pltpu.VMEM(s, d) if keep else jax.ShapeDtypeStruct(s, d) for s, d, keep in outs]
    moved = sum(math.prod(s) * jnp.dtype(d).itemsize for s, d, _ in outs)
    return pl.pallas_call(
        kernel,
        out_shape=shapes,
        in_specs=in_specs,
        out_specs=[pl.BlockSpec(memory_space=pltpu.VMEM)] * len(outs),
        scratch_shapes=list(scratch),
        compiler_params=pltpu.CompilerParams(vmem_limit_bytes=limit),
        cost_estimate=pl.CostEstimate(flops=flops, bytes_accessed=moved, transcendentals=0),
        name=name,
    )


VM = pl.BlockSpec(memory_space=pltpu.VMEM)
ANY = pl.BlockSpec(memory_space=pl.ANY)


def bit_reverse(value, bits):
    out = 0
    for b in range(bits):
        out = out | (((value >> b) & 1) << (bits - 1 - b))
    return out


def slot_masks(near):
    return {0: [], 1: [(1, 1)], 2: [(2, 2), (1, 1), (3, 3)]}[near]


def sum_mask(bit, near):
    return 3 << (bit - 1) if bit == near and near else 1 << bit


def place_of(slot, row_bits, near, share_tiles, group_tiles):
    my_row = lax.axis_index("row")
    my_col = lax.axis_index("col")
    tile_cols = share_tiles << row_bits
    tile_row = lax.div(slot, tile_cols)
    tile_col = lax.rem(slot, tile_cols)
    row_share = lax.div(tile_row, share_tiles)
    apart = row_share ^ my_col
    if near:
        apart = apart ^ (((apart >> near) & 1) << (near - 1))
    mask = apart & ((1 << near) - 1)
    group = mask * 0
    for at, (even, odd) in enumerate(slot_masks(near)):
        group = jnp.where(mask == jnp.where((my_row & 1) == 1, odd, even), at + 1, group)
    row_at = group * group_tiles + (row_share >> near) * share_tiles + lax.rem(tile_row, share_tiles)
    col_share = bit_reverse(lax.div(tile_col, share_tiles) ^ my_row, row_bits)
    return row_at, col_share * share_tiles + lax.rem(tile_col, share_tiles)


def densify(place, tiles_ref, slots_ref, count_ref, dense_ref, held, slots, count, sems):
    copies = [
        pltpu.make_async_copy(count_ref, count, sems.at[0]),
        pltpu.make_async_copy(slots_ref, slots, sems.at[1]),
        pltpu.make_async_copy(tiles_ref.at[0, 0], held, sems.at[2]),
    ]
    for copy in copies:
        copy.start()
    dense_ref[...] = jnp.zeros_like(dense_ref)
    size = held.shape[-1]
    for copy in copies:
        copy.wait()

    def step(k, carry):
        row_at, col_at = place(slots[0, 0, k])
        rows = pl.ds(pl.multiple_of(row_at * size, size), size)
        cols = pl.ds(pl.multiple_of(col_at * size, size), size)
        dense_ref[rows, cols] = held[k]
        return carry

    lax.fori_loop(0, count[0, 0], step, 0)


def forward(parts, *refs):
    dense_ref, pieces, outs = refs[0], refs[1 : 1 + parts], refs[1 + parts :]
    group = outs[0].shape[0]
    for m in [*range(1, len(outs)), 0]:
        total, at = None, 0
        for piece in pieces:
            depth = piece.shape[0]
            term = jnp.dot(
                dense_ref[m * group : (m + 1) * group, at : at + depth], piece[...], preferred_element_type=F32
            )
            total = term if total is None else total + term
            at += depth
        outs[m][...] = total.astype(outs[m].dtype)


def middle(near, share, left_ref, right_ref, weight_ref, *refs):
    cot_refs, (send_ref, hidden_ref, high_ref, low_ref) = refs[:-4], refs[-4:]
    group = high_ref.shape[0]
    place = lax.axis_index("col") >> near
    weight = weight_ref[...]
    at = 0
    for cot_ref in cot_refs:
        for start in range(0, cot_ref.shape[0], share):
            rows = pl.ds(pl.multiple_of((place ^ at) * share, share), share)
            agg = left_ref[rows, :].astype(F32) + right_ref[rows, :].astype(F32)
            high = agg.astype(BF16)
            low = (agg - high.astype(F32)).astype(BF16)
            high_ref[rows, :] = high
            low_ref[rows, :] = low
            summed = jnp.dot(high, weight, preferred_element_type=F32)
            summed += jnp.dot(low, weight, preferred_element_type=F32)
            gate = 1.0 / (1.0 + jnp.exp(-summed))
            if at == 0:
                hidden_ref[...] = (summed * gate).astype(BF16)
            slope = gate * (1.0 + summed * (1.0 - gate))
            send_ref[rows, :] = (cot_ref[start : start + share, :].astype(F32) * slope).astype(BF16)
            at += 1
    dims = (((0,), (0,)), ((), ()))
    grad = send_ref[:group, :]
    term = lax.dot_general(high_ref[...], grad, dims, preferred_element_type=F32)
    term += lax.dot_general(low_ref[...], grad, dims, preferred_element_type=F32)
    send_ref[group:, :] = term.astype(BF16)


def pair_sums(terms):
    while len(terms) > 1:
        terms = [a + b for a, b in zip(terms[::2], terms[1::2])]
    return terms[0]


def backward(dense_ref, *refs):
    grads, (send_ref, keep_ref) = refs[:-2], refs[-2:]
    kept = keep_ref.shape[0]
    group = dense_ref.shape[0] // len(grads)
    dims = (((0,), (0,)), ((), ()))

    def product(cols):
        total = None
        for m, grad in enumerate(grads):
            term = lax.dot_general(
                grad[:group, :], dense_ref[m * group : (m + 1) * group, cols], dims, preferred_element_type=F32
            )
            total = term if total is None else total + term
        return total.T

    send_ref[:kept, :] = product(slice(kept, 2 * kept)).astype(BF16)
    send_ref[kept:, :] = pair_sums([grad[group:, :].astype(F32) for grad in grads]).astype(BF16)
    keep_ref[...] = product(slice(0, kept))


def finish(scale, keep_ref, own_ref, other_ref, weight_ref, grad_ref, wgrad_ref):
    share = keep_ref.shape[0]
    grad_proj = (keep_ref[...] + other_ref[:share, :].astype(F32)).astype(BF16)
    grad_ref[...] = lax.dot_general(
        grad_proj, weight_ref[...], (((1,), (1,)), ((), ())), preferred_element_type=F32
    ).astype(BF16)
    wgrad_ref[...] = (own_ref[share:, :].astype(F32) + other_ref[share:, :].astype(F32)) * scale


def swap(x, axis, mask):
    n = lax.axis_size(axis)
    return lax.ppermute(x, axis, [(i, i ^ mask) for i in range(n)])


def swap_by_row(x, masks):
    row_count, col_count = lax.axis_size("row"), lax.axis_size("col")
    pairs = [
        (r * col_count + c, r * col_count + (c ^ masks[r & 1])) for r in range(row_count) for c in range(col_count)
    ]
    return lax.ppermute(x, ("row", "col"), pairs)


class DenseBlock:
    def __init__(self, place, rows, cols, tiles, tile_slots, tile_counts):
        (self.dense,) = kernel_call(
            functools.partial(densify, place),
            [((rows, cols), BF16, True)],
            0,
            "densify",
            [ANY] * 3,
            [
                pltpu.VMEM(tiles.shape[2:], BF16),
                pltpu.SMEM(tile_slots.shape, jnp.int32),
                pltpu.SMEM(tile_counts.shape, jnp.int32),
                pltpu.SemaphoreType.DMA((3,)),
            ],
        )(in_hbm(tiles), tile_slots, tile_counts)

    def after(self, x):
        x, self.dense = lax.optimization_barrier((x, self.dense))
        return x

    def forward(self, pieces, groups):
        rows, cols = self.dense.shape
        width = pieces[0].shape[-1]
        return kernel_call(
            functools.partial(forward, len(pieces)),
            [((rows // groups, width), BF16 if m else F32, True) for m in range(groups)],
            2 * rows * cols * width,
            "forward",
            [VM] * (1 + len(pieces)),
        )(in_vmem(self.dense), *pieces)

    def backward(self, grads):
        rows, cols = self.dense.shape
        width = grads[0].shape[-1]
        return kernel_call(
            backward,
            [((cols // 2 + width, width), BF16, True), ((cols // 2, width), F32, True)],
            2 * rows * cols * width,
            "backward",
            [VM] * (1 + len(grads)),
        )(in_vmem(self.dense), *grads)


class TiledBlock:
    def __init__(self, place, rows, cols, tiles, tile_slots, tile_counts):
        self.tiles, slots = tiles[0, 0], tile_slots[0, 0]
        self.size = self.tiles.shape[-1]
        self.row_count, self.col_count = rows // self.size, cols // self.size
        self.row_at, self.col_at = place(slots)
        self.live = jnp.arange(slots.shape[0], dtype=jnp.int32) < tile_counts[0, 0]

    def after(self, x):
        return x

    def forward(self, pieces, groups):
        given = jnp.concatenate(pieces).reshape(self.col_count, self.size, -1)[self.col_at]
        terms = jnp.einsum("tij,tjf->tif", self.tiles, given, preferred_element_type=F32)
        at = jnp.where(self.live, self.row_at, self.row_count)
        sums = jax.ops.segment_sum(terms, at, self.row_count + 1)[: self.row_count]
        parts = jnp.split(sums.reshape(-1, given.shape[-1]), groups)
        return [parts[0], *[part.astype(BF16) for part in parts[1:]]]

    def backward(self, grads):
        group = self.row_count * self.size // len(grads)
        given = jnp.concatenate([grad[:group] for grad in grads])
        given = given.reshape(self.row_count, self.size, -1)[self.row_at]
        terms = jnp.einsum("tji,tjf->tif", self.tiles, given, preferred_element_type=F32)
        at = jnp.where(self.live, self.col_at, self.col_count)
        sums = jax.ops.segment_sum(terms, at, self.col_count + 1)[: self.col_count]
        keep, send = jnp.split(sums.reshape(-1, given.shape[-1]), 2)
        wsum = pair_sums([grad[group:].astype(F32) for grad in grads])
        return lax.optimization_barrier(jnp.concatenate([send, wsum]).astype(BF16)), keep


def body(features, weight, tiles, tile_slots, tile_counts, cotangent):
    size = tiles.shape[-1]
    share, width = features.shape
    row_count, col_count = lax.axis_size("row"), lax.axis_size("col")
    row_bits, col_bits = row_count.bit_length() - 1, col_count.bit_length() - 1
    near = min(2, col_bits)
    rows, cols = share * col_count, share * row_count
    group = rows >> near
    place = functools.partial(
        place_of, row_bits=row_bits, near=near, share_tiles=share // size, group_tiles=group // size
    )
    block_type = DenseBlock if 2 * rows * cols <= DENSE_LIMIT else TiledBlock
    block = block_type(place, rows, cols, tiles, tile_slots, tile_counts)

    pieces = [features]
    for bit in reversed(range(row_bits)):
        pieces += [swap(piece, "row", 1 << bit) for piece in pieces]
        if bit == row_bits - 1:
            pieces[1] = block.after(pieces[1])
    total, *sends = block.forward(pieces, 1 << near)

    sends, cotangent = lax.optimization_barrier((sends, cotangent))
    cots = [cotangent]
    for bit in range(near, col_bits):
        cots += [swap(piece, "col", sum_mask(bit, near)) for piece in cots]

    for send, masks in zip(sends, slot_masks(near)):
        total = total + swap_by_row(send, masks).astype(F32)
    left, cots = lax.optimization_barrier((total.astype(BF16), cots))
    right = jnp.zeros_like(left)
    for bit in range(near, col_bits):
        if bit > near:
            left = lax.optimization_barrier((left.astype(F32) + right.astype(F32)).astype(BF16))
        right = swap(left, "col", sum_mask(bit, near))

    grads, hidden = kernel_call(
        functools.partial(middle, near, share),
        [((group + width, width), BF16, True), ((share, width), BF16, False)],
        8 * group * width * width,
        "middle",
        [VM] * (3 + len(cots)),
        [pltpu.VMEM((group, width), BF16)] * 2,
    )(left, right, weight, *cots)
    send, keep = block.backward([grads, *[swap_by_row(grads, masks) for masks in slot_masks(near)]])

    kept = cols // 2
    for bit in range(row_bits):
        other = swap(send, "row", 1 << bit)
        if bit == row_bits - 1:
            break
        keep = keep + other[:kept].astype(F32)
        wsum = send[kept:].astype(F32) + other[kept:].astype(F32)
        kept //= 2
        send = lax.optimization_barrier(jnp.concatenate([keep[kept:].astype(BF16), wsum.astype(BF16)]))
        keep = keep[:kept]

    feature_grad, weight_grad = kernel_call(
        functools.partial(finish, 1.0 / math.sqrt(share * row_count * col_count)),
        [((share, width), BF16, False), ((width, width), F32, False)],
        2 * share * width * width,
        "finish",
        [VM] * 4,
    )(keep, send, other, weight)
    return hidden, feature_grad, weight_grad


def solution(mesh):
    placed = (
        P(("col", "row"), None),
        P(),
        P("row", "col", None, None, None),
        P("row", "col", None),
        P("row", "col"),
        P(("row", "col"), None),
    )
    return jax.shard_map(
        body,
        mesh=mesh,
        in_specs=placed,
        out_specs=(P(("row", "col"), None), P(("col", "row"), None), P()),
        check_vma=False,
    )
```

```python
import functools
import math

import jax
import jax.numpy as jnp
from jax import lax
from jax.experimental import pallas as pl
from jax.experimental.pallas import tpu as pltpu
from jax.sharding import PartitionSpec as P

F32 = jnp.float32
BF16 = jnp.bfloat16
VMEM_LIMIT = 24 * 1024 * 1024
DENSE_LIMIT = 12 * 1024 * 1024


def in_vmem(x):
    return pltpu.with_memory_space_constraint(x, pltpu.VMEM)


def in_hbm(x):
    return pltpu.with_memory_space_constraint(x, pltpu.HBM)


def kernel_call(kernel, outs, flops, name, in_specs, scratch=(), limit=VMEM_LIMIT):
    shapes = [pltpu.VMEM(s, d) if keep else jax.ShapeDtypeStruct(s, d) for s, d, keep in outs]
    moved = sum(math.prod(s) * jnp.dtype(d).itemsize for s, d, _ in outs)
    return pl.pallas_call(
        kernel,
        out_shape=shapes,
        in_specs=in_specs,
        out_specs=[pl.BlockSpec(memory_space=pltpu.VMEM)] * len(outs),
        scratch_shapes=list(scratch),
        compiler_params=pltpu.CompilerParams(vmem_limit_bytes=limit),
        cost_estimate=pl.CostEstimate(flops=flops, bytes_accessed=moved, transcendentals=0),
        name=name,
    )


SPLIT = True
VM = pl.BlockSpec(memory_space=pltpu.VMEM)
ANY = pl.BlockSpec(memory_space=pl.ANY)


def bit_reverse(value, bits):
    out = 0
    for b in range(bits):
        out = out | (((value >> b) & 1) << (bits - 1 - b))
    return out


PARTNERS = {0: [], 1: [1], 2: [2, 1, 3]}


def sum_mask(bit, near):
    return 3 << (bit - 1) if bit == near and near else 1 << bit


def quotient(value, by):
    if by & (by - 1):
        return lax.div(value, by), lax.rem(value, by)
    return value >> (by.bit_length() - 1), value & (by - 1)


def place_of(slot, my_row, my_col, row_bits, near, share_tiles, group_tiles):
    tile_row, tile_col = quotient(slot, share_tiles << row_bits)
    row_share, row_rest = quotient(tile_row, share_tiles)
    col_share, col_rest = quotient(tile_col, share_tiles)
    apart = row_share ^ my_col
    if near:
        apart = apart ^ (((apart >> near) & 1) << (near - 1))
    mask = apart & ((1 << near) - 1)
    group = mask * 0
    for at, partner in enumerate(PARTNERS[near]):
        group = jnp.where(mask == partner, at + 1, group)
    row_at = group * group_tiles + (row_share >> near) * share_tiles + row_rest
    return row_at, bit_reverse(col_share ^ my_row, row_bits) * share_tiles + col_rest


def densify(place, parts, tiles_ref, slots_ref, count_ref, dense_ref, held, slots, sems):
    total, size, _ = held.shape
    step = -(-total // parts)
    copies = [pltpu.make_async_copy(slots_ref, slots, sems.at[parts])]
    for part, start in enumerate(range(0, total, step)):
        some = pl.ds(start, min(step, total - start))
        copies.append(pltpu.make_async_copy(tiles_ref.at[0, 0, some], held.at[some], sems.at[part]))
    for copy in copies:
        copy.start()
    dense_ref[...] = jnp.zeros_like(dense_ref)
    my_row, my_col = lax.axis_index("row"), lax.axis_index("col")
    dead = dense_ref.shape[0] // size - 1
    count = count_ref[0, 0]
    for copy in copies:
        copy.wait()
    unroll = 4

    def some_tiles(first, carry):
        for inner in range(unroll):
            k = jnp.minimum(first * unroll + inner, total - 1)
            row_at, col_at = place(slots[0, 0, k], my_row, my_col)
            row_at = jnp.where(first * unroll + inner < count, row_at, dead)
            rows = pl.ds(pl.multiple_of(row_at * size, size), size)
            cols = pl.ds(pl.multiple_of(col_at * size, size), size)
            dense_ref[rows, cols] = held[k]
        return carry

    lax.fori_loop(0, (count + unroll - 1) // unroll, some_tiles, 0)


def forward(parts, groups, *refs):
    dense_ref, pieces, outs = refs[0], refs[1 : 1 + parts], refs[1 + parts :]
    for m, ref in zip(groups, outs):
        group, total, at = ref.shape[0], None, 0
        for piece in pieces:
            depth = piece.shape[0]
            term = jnp.dot(
                dense_ref[m * group : (m + 1) * group, at : at + depth], piece[...], preferred_element_type=F32
            )
            total = term if total is None else total + term
            at += depth
        ref[...] = total.astype(ref.dtype)


def middle(near, share, left_ref, right_ref, weight_ref, *refs):
    cot_refs, (send_ref, hidden_ref, agg_ref) = refs[:-3], refs[-3:]
    group, width = agg_ref.shape[0], left_ref.shape[1]
    place = lax.axis_index("col") >> near
    weight = jnp.concatenate([weight_ref[...]] * 2)
    at = 0
    for cot_ref in cot_refs:
        for start in range(0, cot_ref.shape[0], share):
            rows = pl.ds(pl.multiple_of((place ^ at) * share, share), share)
            agg = left_ref[rows, :].astype(F32) + right_ref[rows, :].astype(F32)
            high = agg.astype(BF16)
            both = jnp.concatenate([high, (agg - high.astype(F32)).astype(BF16)], axis=1)
            agg_ref[rows, :] = both
            summed = jnp.dot(both, weight, preferred_element_type=F32)
            gate = 1.0 / (1.0 + jnp.exp(-summed))
            if at == 0:
                hidden_ref[...] = (summed * gate).astype(BF16)
            slope = gate * (1.0 + summed * (1.0 - gate))
            send_ref[rows, :] = (cot_ref[start : start + share, :].astype(F32) * slope).astype(BF16)
            at += 1
    term = lax.dot_general(
        send_ref[:group, :], agg_ref[...], (((0,), (0,)), ((), ())), preferred_element_type=F32
    )
    send_ref[group:, :] = (term[:, :width] + term[:, width:]).T.astype(BF16)


def emit(given_ref, out_ref):
    out_ref[...] = given_ref[...]


def pair_sums(terms):
    while len(terms) > 1:
        terms = [a + b for a, b in zip(terms[::2], terms[1::2])]
    return terms[0]


def columns_of(dense_ref, grads, first, columns):
    total = None
    for m, grad in enumerate(grads, first):
        group = grad.shape[0] - grad.shape[1]
        term = lax.dot_general(
            grad[:group, :],
            dense_ref[m * group : (m + 1) * group, columns],
            (((0,), (0,)), ((), ())),
            preferred_element_type=F32,
        )
        total = term if total is None else total + term
    return total


def backward_own(dense_ref, grad_ref, total_ref):
    total_ref[...] = columns_of(dense_ref, [grad_ref], 0, slice(0, total_ref.shape[1]))


def backward_sent(dense_ref, total_ref, *refs):
    grads, send_ref = refs[:-1], refs[-1]
    kept = total_ref.shape[1] // 2
    columns = slice(kept, 2 * kept)
    send_ref[:kept, :] = (columns_of(dense_ref, grads[1:], 1, columns) + total_ref[:, columns]).T.astype(BF16)
    send_ref[kept:, :] = pair_sums([grad[-grad.shape[1] :, :].astype(F32) for grad in grads]).astype(BF16)


def backward_kept(dense_ref, total_ref, *refs):
    grads, keep_ref = refs[:-1], refs[-1]
    columns = slice(0, keep_ref.shape[0])
    keep_ref[...] = (columns_of(dense_ref, grads, 1, columns) + total_ref[:, columns]).T


def finish(scale, keep_ref, own_ref, other_ref, weight_ref, grad_ref, wgrad_ref):
    share = keep_ref.shape[0]
    grad_proj = (keep_ref[...] + other_ref[:share, :].astype(F32)).astype(BF16)
    grad_ref[...] = lax.dot_general(
        grad_proj, weight_ref[...], (((1,), (1,)), ((), ())), preferred_element_type=F32
    ).astype(BF16)
    wgrad_ref[...] = (own_ref[share:, :].astype(F32) + other_ref[share:, :].astype(F32)) * scale


def swap(x, axis, mask):
    n = lax.axis_size(axis)
    return lax.ppermute(x, axis, [(i, i ^ mask) for i in range(n)])


class DenseBlock:
    def __init__(self, place, rows, cols, tiles, tile_slots, tile_counts):
        (self.dense,) = kernel_call(
            functools.partial(densify, place, 4),
            [((rows + tiles.shape[-1], cols), BF16, True)],
            0,
            "densify",
            [ANY, ANY, pl.BlockSpec(memory_space=pltpu.SMEM)],
            [
                pltpu.VMEM(tiles.shape[2:], BF16),
                pltpu.SMEM(tile_slots.shape, jnp.int32),
                pltpu.SemaphoreType.DMA((5,)),
            ],
        )(in_hbm(tiles), in_hbm(tile_slots), tile_counts)
        self.rows, self.cols = rows, cols

    def after(self, x):
        x, self.dense = lax.optimization_barrier((x, self.dense))
        return x

    def forward(self, pieces, groups):
        width, group = pieces[0].shape[-1], self.rows // groups

        def some(name, which, dtype):
            return kernel_call(
                functools.partial(forward, len(pieces), which),
                [((group, width), dtype, True) for _ in which],
                2 * len(which) * group * self.cols * width,
                name,
                [VM] * (1 + len(pieces)),
            )(in_vmem(self.dense), *pieces)

        sends = some("forward_sent", range(1, groups), BF16) if groups > 1 else []
        if SPLIT:
            (self.dense, sends) = lax.optimization_barrier((self.dense, sends))
        return [*some("forward_own", [0], F32), *sends]

    def backward(self, grads):
        rows, cols = self.rows, self.cols
        width = grads[0].shape[-1]
        dense = in_vmem(self.dense)

        def some(kernel, shape, dtype, flops, name, *given):
            (out,) = kernel_call(kernel, [(shape, dtype, True)], flops, name, [VM] * (1 + len(given)))(dense, *given)
            return out

        flops = 2 * rows * cols * width // len(grads)
        total = some(backward_own, (width, cols), F32, flops, "backward_own", grads[0])
        flops = 2 * rows * cols * width // 2
        send = some(backward_sent, (cols // 2 + width, width), BF16, flops, "backward_sent", total, *grads)
        return send, some(backward_kept, (cols // 2, width), F32, flops, "backward_kept", total, *grads[1:])


class TiledBlock:
    def __init__(self, place, rows, cols, tiles, tile_slots, tile_counts):
        self.tiles, slots = tiles[0, 0], tile_slots[0, 0]
        self.size = self.tiles.shape[-1]
        self.row_count, self.col_count = rows // self.size, cols // self.size
        self.row_at, self.col_at = place(slots, lax.axis_index("row"), lax.axis_index("col"))
        self.live = jnp.arange(slots.shape[0], dtype=jnp.int32) < tile_counts[0, 0]

    def after(self, x):
        return x

    def forward(self, pieces, groups):
        given = jnp.concatenate(pieces).reshape(self.col_count, self.size, -1)[self.col_at]
        terms = jnp.einsum("tij,tjf->tif", self.tiles, given, preferred_element_type=F32)
        at = jnp.where(self.live, self.row_at, self.row_count)
        sums = jax.ops.segment_sum(terms, at, self.row_count + 1)[: self.row_count]
        parts = jnp.split(sums.reshape(-1, given.shape[-1]), groups)
        return [parts[0], *[part.astype(BF16) for part in parts[1:]]]

    def backward(self, grads):
        group = self.row_count * self.size // len(grads)
        given = jnp.concatenate([grad[:group] for grad in grads])
        given = given.reshape(self.row_count, self.size, -1)[self.row_at]
        terms = jnp.einsum("tji,tjf->tif", self.tiles, given, preferred_element_type=F32)
        at = jnp.where(self.live, self.col_at, self.col_count)
        sums = jax.ops.segment_sum(terms, at, self.col_count + 1)[: self.col_count]
        keep, send = jnp.split(sums.reshape(-1, given.shape[-1]), 2)
        wsum = pair_sums([grad[group:].astype(F32) for grad in grads])
        return lax.optimization_barrier(jnp.concatenate([send, wsum]).astype(BF16)), keep


def body(features, weight, tiles, tile_slots, tile_counts, cotangent):
    size = tiles.shape[-1]
    share, width = features.shape
    row_count, col_count = lax.axis_size("row"), lax.axis_size("col")
    row_bits, col_bits = row_count.bit_length() - 1, col_count.bit_length() - 1
    near = min(2, col_bits)
    rows, cols = share * col_count, share * row_count
    group = rows >> near
    place = functools.partial(
        place_of, row_bits=row_bits, near=near, share_tiles=share // size, group_tiles=group // size
    )
    block_type = DenseBlock if 2 * rows * cols <= DENSE_LIMIT else TiledBlock
    block = block_type(place, rows, cols, tiles, tile_slots, tile_counts)

    pieces = [features]
    for bit in reversed(range(row_bits)):
        pieces += [swap(piece, "row", 1 << bit) for piece in pieces]
        if bit == row_bits - 1:
            pieces[1] = block.after(pieces[1])
    total, *sends = block.forward(pieces, 1 << near)

    sends, cotangent = lax.optimization_barrier((sends, cotangent))
    cots = [cotangent]
    for bit in range(near, col_bits):
        cots += [swap(piece, "col", sum_mask(bit, near)) for piece in cots]

    for send, mask in zip(sends, PARTNERS[near]):
        total = total + swap(send, "col", mask).astype(F32)
    left, cots = lax.optimization_barrier((total.astype(BF16), cots))
    right = jnp.zeros_like(left)
    for bit in range(near, col_bits):
        if bit > near:
            left = lax.optimization_barrier((left.astype(F32) + right.astype(F32)).astype(BF16))
        right = swap(left, "col", sum_mask(bit, near))

    grads, hidden = kernel_call(
        functools.partial(middle, near, share),
        [((group + width, width), BF16, True), ((share, width), BF16, True)],
        8 * group * width * width,
        "middle",
        [VM] * (3 + len(cots)),
        [pltpu.VMEM((group, 2 * width), BF16)],
    )(left, right, weight, *cots)
    (hidden,) = kernel_call(emit, [((share, width), BF16, False)], 0, "emit", [VM])(hidden)
    send, keep = block.backward([grads, *[swap(grads, "col", mask) for mask in PARTNERS[near]]])

    kept = cols // 2
    for bit in range(row_bits):
        other = swap(send, "row", 1 << bit)
        if bit == row_bits - 1:
            break
        keep = keep + other[:kept].astype(F32)
        wsum = send[kept:].astype(F32) + other[kept:].astype(F32)
        kept //= 2
        send = lax.optimization_barrier(jnp.concatenate([keep[kept:].astype(BF16), wsum.astype(BF16)]))
        keep = keep[:kept]

    feature_grad, weight_grad = kernel_call(
        functools.partial(finish, 1.0 / math.sqrt(share * row_count * col_count)),
        [((share, width), BF16, False), ((width, width), F32, False)],
        2 * share * width * width,
        "finish",
        [VM] * 4,
    )(keep, send, other, weight)
    return hidden, feature_grad, weight_grad


def solution(mesh):
    placed = (
        P(("col", "row"), None),
        P(),
        P("row", "col", None, None, None),
        P("row", "col", None),
        P("row", "col"),
        P(("row", "col"), None),
    )
    return jax.shard_map(
        body,
        mesh=mesh,
        in_specs=placed,
        out_specs=(P(("row", "col"), None), P(("col", "row"), None), P()),
        check_vma=False,
    )
```

```python
import functools
import math

import jax
import jax.numpy as jnp
from jax import lax
from jax.experimental import pallas as pl
from jax.experimental.pallas import tpu as pltpu
from jax.sharding import PartitionSpec as P

F32 = jnp.float32
BF16 = jnp.bfloat16
VMEM_LIMIT = 24 * 1024 * 1024
DENSIFY_PARTS = 6
DENSE_LIMIT = 12 * 1024 * 1024


def in_vmem(x):
    return pltpu.with_memory_space_constraint(x, pltpu.VMEM)


def in_hbm(x):
    return pltpu.with_memory_space_constraint(x, pltpu.HBM)


def kernel_call(kernel, outs, flops, name, in_specs, scratch=(), limit=VMEM_LIMIT):
    shapes = [pltpu.VMEM(s, d) if keep else jax.ShapeDtypeStruct(s, d) for s, d, keep in outs]
    moved = sum(math.prod(s) * jnp.dtype(d).itemsize for s, d, _ in outs)
    return pl.pallas_call(
        kernel,
        out_shape=shapes,
        in_specs=in_specs,
        out_specs=[pl.BlockSpec(memory_space=pltpu.VMEM)] * len(outs),
        scratch_shapes=list(scratch),
        compiler_params=pltpu.CompilerParams(vmem_limit_bytes=limit),
        cost_estimate=pl.CostEstimate(flops=flops, bytes_accessed=moved, transcendentals=0),
        name=name,
    )


VM = pl.BlockSpec(memory_space=pltpu.VMEM)
ANY = pl.BlockSpec(memory_space=pl.ANY)


def bit_reverse(value, bits):
    out = 0
    for b in range(bits):
        out = out | (((value >> b) & 1) << (bits - 1 - b))
    return out


PARTNERS = {0: [], 1: [1], 2: [2, 1, 3]}


def sum_mask(bit, near):
    return 3 << (bit - 1) if bit == near and near else 1 << bit


def quotient(value, by):
    if by & (by - 1):
        return lax.div(value, by), lax.rem(value, by)
    return value >> (by.bit_length() - 1), value & (by - 1)


def row_place(tile_row, my_col, near, share_tiles, group_tiles):
    share, rest = quotient(tile_row, share_tiles)
    apart = share ^ my_col
    if near:
        apart = apart ^ (((apart >> near) & 1) << (near - 1))
    mask = apart & ((1 << near) - 1)
    group = mask * 0
    for at, partner in enumerate(PARTNERS[near]):
        group = jnp.where(mask == partner, at + 1, group)
    return group * group_tiles + (share >> near) * share_tiles + rest


def col_place(tile_col, my_row, row_bits, share_tiles):
    share, rest = quotient(tile_col, share_tiles)
    return bit_reverse(share ^ my_row, row_bits) * share_tiles + rest


def densify(row_of, col_of, parts, tiles_ref, slots_ref, count_ref, dense_ref, held, slots, row_at, col_at, sems):
    total, size, _ = held.shape
    step = -(-total // parts)
    copies = [pltpu.make_async_copy(slots_ref, slots, sems.at[parts])]
    for part, start in enumerate(range(0, total, step)):
        some = pl.ds(start, min(step, total - start))
        copies.append(pltpu.make_async_copy(tiles_ref.at[0, 0, some], held.at[some], sems.at[part]))
    for copy in copies:
        copy.start()
    dense_ref[...] = jnp.zeros_like(dense_ref)
    my_row, my_col = lax.axis_index("row"), lax.axis_index("col")
    for at in range(row_at.shape[0]):
        row_at[at] = row_of(jnp.int32(at), my_col) * size
    for at in range(col_at.shape[0]):
        col_at[at] = col_of(jnp.int32(at), my_row) * size
    dead = dense_ref.shape[0] - size
    count = count_ref[0, 0]
    copies[0].wait()
    unroll = 4
    for copy, start in zip(copies[1:], range(0, total, step)):
        end = min(start + step, total)
        copy.wait()

        def some_tiles(turn, carry, start=start, end=end):
            for inner in range(unroll):
                k = start + turn * unroll + inner
                at = jnp.minimum(k, end - 1)
                tile_row, tile_col = quotient(slots[0, 0, at], col_at.shape[0])
                row = jnp.where((k < count) & (k < end), row_at[tile_row], dead)
                rows = pl.ds(pl.multiple_of(row, size), size)
                cols = pl.ds(pl.multiple_of(col_at[tile_col], size), size)
                dense_ref[rows, cols] = held[at]
            return carry

        turns = (jnp.clip(count - start, 0, end - start) + unroll - 1) // unroll
        lax.fori_loop(0, turns, some_tiles, 0)


def rows_of(dense_ref, pieces, first, step, rows):
    total = None
    for at, piece in enumerate(pieces):
        depth = piece.shape[0]
        start = (first + at * step) * depth
        term = jnp.dot(dense_ref[rows, start : start + depth], piece[...], preferred_element_type=F32)
        total = term if total is None else total + term
    return total


def forward_early(sent, dense_ref, *refs):
    pieces, total_ref = refs[:-1], refs[-1]
    rows = total_ref.shape[0]
    group = rows // sent
    total_ref[...] = rows_of(dense_ref, pieces, 0, 2, slice(group, group + rows))


def forward_sent(parts, dense_ref, total_ref, *refs):
    pieces, outs = refs[:parts], refs[parts:]
    for m, ref in enumerate(outs):
        group = ref.shape[0]
        total = rows_of(dense_ref, pieces, 1, 2, slice((m + 1) * group, (m + 2) * group))
        ref[...] = (total + total_ref[m * group : (m + 1) * group, :]).astype(BF16)


def forward_own(dense_ref, *refs):
    pieces, out_ref = refs[:-1], refs[-1]
    out_ref[...] = rows_of(dense_ref, pieces, 0, 1, slice(0, out_ref.shape[0]))


def middle(near, share, left_ref, right_ref, weight_ref, *refs):
    cot_refs, (send_ref, hidden_ref, agg_ref) = refs[:-3], refs[-3:]
    group, width = agg_ref.shape[0], left_ref.shape[1]
    place = lax.axis_index("col") >> near
    weight = jnp.concatenate([weight_ref[...]] * 2)
    at = 0
    for cot_ref in cot_refs:
        for start in range(0, cot_ref.shape[0], share):
            rows = pl.ds(pl.multiple_of((place ^ at) * share, share), share)
            agg = left_ref[rows, :].astype(F32) + right_ref[rows, :].astype(F32)
            high = agg.astype(BF16)
            both = jnp.concatenate([high, (agg - high.astype(F32)).astype(BF16)], axis=1)
            agg_ref[rows, :] = both
            summed = jnp.dot(both, weight, preferred_element_type=F32)
            gate = 1.0 / (1.0 + jnp.exp(-summed))
            if at == 0:
                hidden_ref[...] = (summed * gate).astype(BF16)
            slope = gate * (1.0 + summed * (1.0 - gate))
            send_ref[rows, :] = (cot_ref[start : start + share, :].astype(F32) * slope).astype(BF16)
            at += 1
    term = lax.dot_general(
        send_ref[:group, :], agg_ref[...], (((0,), (0,)), ((), ())), preferred_element_type=F32
    )
    send_ref[group:, :] = (term[:, :width] + term[:, width:]).T.astype(BF16)


def emit(given_ref, out_ref):
    out_ref[...] = given_ref[...]


def pair_sums(terms):
    while len(terms) > 1:
        terms = [a + b for a, b in zip(terms[::2], terms[1::2])]
    return terms[0]


def columns_of(dense_ref, grads, first, columns):
    total = None
    for m, grad in enumerate(grads, first):
        group = grad.shape[0] - grad.shape[1]
        term = lax.dot_general(
            grad[:group, :],
            dense_ref[m * group : (m + 1) * group, columns],
            (((0,), (0,)), ((), ())),
            preferred_element_type=F32,
        )
        total = term if total is None else total + term
    return total


def backward_own(dense_ref, grad_ref, total_ref):
    total_ref[...] = columns_of(dense_ref, [grad_ref], 0, slice(0, total_ref.shape[1]))


def backward_sent(dense_ref, total_ref, *refs):
    grads, send_ref = refs[:-1], refs[-1]
    kept = total_ref.shape[1] // 2
    columns = slice(kept, 2 * kept)
    send_ref[:kept, :] = (columns_of(dense_ref, grads[1:], 1, columns) + total_ref[:, columns]).T.astype(BF16)
    send_ref[kept:, :] = pair_sums([grad[-grad.shape[1] :, :].astype(F32) for grad in grads]).astype(BF16)


def backward_kept(dense_ref, total_ref, *refs):
    grads, keep_ref = refs[:-1], refs[-1]
    columns = slice(0, keep_ref.shape[0])
    keep_ref[...] = (columns_of(dense_ref, grads, 1, columns) + total_ref[:, columns]).T


def finish(scale, keep_ref, own_ref, other_ref, weight_ref, grad_ref, wgrad_ref):
    share = keep_ref.shape[0]
    grad_proj = (keep_ref[...] + other_ref[:share, :].astype(F32)).astype(BF16)
    grad_ref[...] = lax.dot_general(
        grad_proj, weight_ref[...], (((1,), (1,)), ((), ())), preferred_element_type=F32
    ).astype(BF16)
    wgrad_ref[...] = (own_ref[share:, :].astype(F32) + other_ref[share:, :].astype(F32)) * scale


def swap(x, axis, mask):
    n = lax.axis_size(axis)
    return lax.ppermute(x, axis, [(i, i ^ mask) for i in range(n)])


class DenseBlock:
    def __init__(self, row_of, col_of, rows, cols, tiles, tile_slots, tile_counts):
        (self.dense,) = kernel_call(
            functools.partial(densify, row_of, col_of, DENSIFY_PARTS),
            [((rows + tiles.shape[-1], cols), BF16, True)],
            0,
            "densify",
            [ANY, ANY, pl.BlockSpec(memory_space=pltpu.SMEM)],
            [
                pltpu.VMEM(tiles.shape[2:], BF16),
                pltpu.SMEM(tile_slots.shape, jnp.int32),
                pltpu.SMEM((rows // tiles.shape[-1],), jnp.int32),
                pltpu.SMEM((cols // tiles.shape[-1],), jnp.int32),
                pltpu.SemaphoreType.DMA((DENSIFY_PARTS + 1,)),
            ],
        )(in_hbm(tiles), in_hbm(tile_slots), tile_counts)
        self.rows, self.cols = rows, cols

    def after(self, x):
        x, self.dense = lax.optimization_barrier((x, self.dense))
        return x

    def forward(self, pieces, groups):
        width, group = pieces[0].shape[-1], self.rows // groups
        sent = groups - 1
        dense = in_vmem(self.dense)
        flops = 2 * group * self.cols * width

        def some(kernel, outs, flops, name, *given):
            return kernel_call(kernel, outs, flops, name, [VM] * (1 + len(given)))(dense, *given)

        (total,) = some(
            functools.partial(forward_early, sent), [((sent * group, width), F32, True)], flops * sent // 2, "forward_early", *pieces[::2]
        )
        late = pieces[1::2]
        sends = some(
            functools.partial(forward_sent, len(late)),
            [((group, width), BF16, True)] * sent,
            flops * sent // 2,
            "forward_sent",
            total,
            *late,
        )
        (own,) = some(forward_own, [((group, width), F32, True)], flops, "forward_own", *pieces)
        return [own, *sends]

    def backward(self, grads):
        rows, cols = self.rows, self.cols
        width = grads[0].shape[-1]
        dense = in_vmem(self.dense)

        def some(kernel, shape, dtype, flops, name, *given):
            (out,) = kernel_call(kernel, [(shape, dtype, True)], flops, name, [VM] * (1 + len(given)))(dense, *given)
            return out

        flops = 2 * rows * cols * width // len(grads)
        total = some(backward_own, (width, cols), F32, flops, "backward_own", grads[0])
        flops = 2 * rows * cols * width // 2
        send = some(backward_sent, (cols // 2 + width, width), BF16, flops, "backward_sent", total, *grads)
        return send, some(backward_kept, (cols // 2, width), F32, flops, "backward_kept", total, *grads[1:])


class TiledBlock:
    def __init__(self, row_of, col_of, rows, cols, tiles, tile_slots, tile_counts):
        self.tiles, slots = tiles[0, 0], tile_slots[0, 0]
        self.size = self.tiles.shape[-1]
        self.row_count, self.col_count = rows // self.size, cols // self.size
        tile_row, tile_col = quotient(slots, self.col_count)
        self.row_at = row_of(tile_row, lax.axis_index("col"))
        self.col_at = col_of(tile_col, lax.axis_index("row"))
        self.live = jnp.arange(slots.shape[0], dtype=jnp.int32) < tile_counts[0, 0]

    def after(self, x):
        return x

    def forward(self, pieces, groups):
        given = jnp.concatenate(pieces).reshape(self.col_count, self.size, -1)[self.col_at]
        terms = jnp.einsum("tij,tjf->tif", self.tiles, given, preferred_element_type=F32)
        at = jnp.where(self.live, self.row_at, self.row_count)
        sums = jax.ops.segment_sum(terms, at, self.row_count + 1)[: self.row_count]
        parts = jnp.split(sums.reshape(-1, given.shape[-1]), groups)
        return [parts[0], *[part.astype(BF16) for part in parts[1:]]]

    def backward(self, grads):
        group = self.row_count * self.size // len(grads)
        given = jnp.concatenate([grad[:group] for grad in grads])
        given = given.reshape(self.row_count, self.size, -1)[self.row_at]
        terms = jnp.einsum("tji,tjf->tif", self.tiles, given, preferred_element_type=F32)
        at = jnp.where(self.live, self.col_at, self.col_count)
        sums = jax.ops.segment_sum(terms, at, self.col_count + 1)[: self.col_count]
        keep, send = jnp.split(sums.reshape(-1, given.shape[-1]), 2)
        wsum = pair_sums([grad[group:].astype(F32) for grad in grads])
        return lax.optimization_barrier(jnp.concatenate([send, wsum]).astype(BF16)), keep


def body(features, weight, tiles, tile_slots, tile_counts, cotangent):
    size = tiles.shape[-1]
    share, width = features.shape
    row_count, col_count = lax.axis_size("row"), lax.axis_size("col")
    row_bits, col_bits = row_count.bit_length() - 1, col_count.bit_length() - 1
    near = min(2, col_bits)
    rows, cols = share * col_count, share * row_count
    group = rows >> near
    row_of = functools.partial(row_place, near=near, share_tiles=share // size, group_tiles=group // size)
    col_of = functools.partial(col_place, row_bits=row_bits, share_tiles=share // size)
    block_type = DenseBlock if 2 * rows * cols <= DENSE_LIMIT else TiledBlock
    block = block_type(row_of, col_of, rows, cols, tiles, tile_slots, tile_counts)

    pieces = [features]
    for bit in reversed(range(row_bits)):
        pieces += [swap(piece, "row", 1 << bit) for piece in pieces]
        if bit == row_bits - 1:
            pieces[1] = block.after(pieces[1])
    total, *sends = block.forward(pieces, 1 << near)

    sends, cotangent = lax.optimization_barrier((sends, cotangent))
    cots = [cotangent]
    for bit in range(near, col_bits):
        cots += [swap(piece, "col", sum_mask(bit, near)) for piece in cots]

    for send, mask in zip(sends, PARTNERS[near]):
        total = total + swap(send, "col", mask).astype(F32)
    left, cots = lax.optimization_barrier((total.astype(BF16), cots))
    right = jnp.zeros_like(left)
    for bit in range(near, col_bits):
        if bit > near:
            left = lax.optimization_barrier((left.astype(F32) + right.astype(F32)).astype(BF16))
        right = swap(left, "col", sum_mask(bit, near))

    grads, hidden = kernel_call(
        functools.partial(middle, near, share),
        [((group + width, width), BF16, True), ((share, width), BF16, True)],
        8 * group * width * width,
        "middle",
        [VM] * (3 + len(cots)),
        [pltpu.VMEM((group, 2 * width), BF16)],
    )(left, right, weight, *cots)
    (hidden,) = kernel_call(emit, [((share, width), BF16, False)], 0, "emit", [VM])(hidden)
    send, keep = block.backward([grads, *[swap(grads, "col", mask) for mask in PARTNERS[near]]])

    kept = cols // 2
    for bit in range(row_bits):
        other = swap(send, "row", 1 << bit)
        if bit == row_bits - 1:
            break
        keep = keep + other[:kept].astype(F32)
        wsum = send[kept:].astype(F32) + other[kept:].astype(F32)
        kept //= 2
        send = lax.optimization_barrier(jnp.concatenate([keep[kept:].astype(BF16), wsum.astype(BF16)]))
        keep = keep[:kept]

    feature_grad, weight_grad = kernel_call(
        functools.partial(finish, 1.0 / math.sqrt(share * row_count * col_count)),
        [((share, width), BF16, False), ((width, width), F32, False)],
        2 * share * width * width,
        "finish",
        [VM] * 4,
    )(keep, send, other, weight)
    return hidden, feature_grad, weight_grad


def solution(mesh):
    placed = (
        P(("col", "row"), None),
        P(),
        P("row", "col", None, None, None),
        P("row", "col", None),
        P("row", "col"),
        P(("row", "col"), None),
    )
    return jax.shard_map(
        body,
        mesh=mesh,
        in_specs=placed,
        out_specs=(P(("row", "col"), None), P(("col", "row"), None), P()),
        check_vma=False,
    )
```

```python
import functools
import math

import jax
import jax.numpy as jnp
from jax import lax
from jax.experimental import pallas as pl
from jax.experimental.pallas import tpu as pltpu
from jax.sharding import PartitionSpec as P

F32 = jnp.float32
BF16 = jnp.bfloat16
VMEM_LIMIT = 24 * 1024 * 1024
DENSIFY_PARTS = 6
DENSE_LIMIT = 12 * 1024 * 1024


def in_vmem(x):
    return pltpu.with_memory_space_constraint(x, pltpu.VMEM)


def in_hbm(x):
    return pltpu.with_memory_space_constraint(x, pltpu.HBM)


def kernel_call(kernel, outs, flops, name, in_specs, scratch=(), limit=VMEM_LIMIT):
    shapes = [pltpu.VMEM(s, d) if keep else jax.ShapeDtypeStruct(s, d) for s, d, keep in outs]
    moved = sum(math.prod(s) * jnp.dtype(d).itemsize for s, d, _ in outs)
    return pl.pallas_call(
        kernel,
        out_shape=shapes,
        in_specs=in_specs,
        out_specs=[pl.BlockSpec(memory_space=pltpu.VMEM)] * len(outs),
        scratch_shapes=list(scratch),
        compiler_params=pltpu.CompilerParams(vmem_limit_bytes=limit),
        cost_estimate=pl.CostEstimate(flops=flops, bytes_accessed=moved, transcendentals=0),
        name=name,
    )


VM = pl.BlockSpec(memory_space=pltpu.VMEM)
ANY = pl.BlockSpec(memory_space=pl.ANY)


def bit_reverse(value, bits):
    out = 0
    for b in range(bits):
        out = out | (((value >> b) & 1) << (bits - 1 - b))
    return out


PARTNERS = {0: [], 1: [1], 2: [2, 1, 3]}


def sum_mask(bit, near):
    return 3 << (bit - 1) if bit == near and near else 1 << bit


def quotient(value, by):
    if by & (by - 1):
        return lax.div(value, by), lax.rem(value, by)
    return value >> (by.bit_length() - 1), value & (by - 1)


def row_place(tile_row, my_col, near, share_tiles, group_tiles):
    share, rest = quotient(tile_row, share_tiles)
    apart = share ^ my_col
    if near:
        apart = apart ^ (((apart >> near) & 1) << (near - 1))
    mask = apart & ((1 << near) - 1)
    group = mask * 0
    for at, partner in enumerate(PARTNERS[near]):
        group = jnp.where(mask == partner, at + 1, group)
    return group * group_tiles + (share >> near) * share_tiles + rest


def col_place(tile_col, my_row, row_bits, share_tiles):
    share, rest = quotient(tile_col, share_tiles)
    return bit_reverse(share ^ my_row, row_bits) * share_tiles + rest


def densify(row_of, col_of, parts, tiles_ref, slots_ref, count_ref, dense_ref, held, slots, row_at, col_at, sems):
    total, size, _ = held.shape
    step = -(-total // parts)
    copies = [pltpu.make_async_copy(slots_ref, slots, sems.at[parts])]
    for part, start in enumerate(range(0, total, step)):
        some = pl.ds(start, min(step, total - start))
        copies.append(pltpu.make_async_copy(tiles_ref.at[0, 0, some], held.at[some], sems.at[part]))
    for copy in copies:
        copy.start()
    dense_ref[...] = jnp.zeros_like(dense_ref)
    my_row, my_col = lax.axis_index("row"), lax.axis_index("col")
    for at in range(row_at.shape[0]):
        row_at[at] = row_of(jnp.int32(at), my_col) * size
    for at in range(col_at.shape[0]):
        col_at[at] = col_of(jnp.int32(at), my_row) * size
    dead = dense_ref.shape[0] - size
    count = count_ref[0, 0]
    copies[0].wait()
    unroll = 4
    for copy, start in zip(copies[1:], range(0, total, step)):
        end = min(start + step, total)
        copy.wait()

        def some_tiles(turn, carry, start=start, end=end):
            for inner in range(unroll):
                k = start + turn * unroll + inner
                at = jnp.minimum(k, end - 1)
                tile_row, tile_col = quotient(slots[0, 0, at], col_at.shape[0])
                row = jnp.where((k < count) & (k < end), row_at[tile_row], dead)
                rows = pl.ds(pl.multiple_of(row, size), size)
                cols = pl.ds(pl.multiple_of(col_at[tile_col], size), size)
                dense_ref[rows, cols] = held[at]
            return carry

        turns = (jnp.clip(count - start, 0, end - start) + unroll - 1) // unroll
        lax.fori_loop(0, turns, some_tiles, 0)


def rows_of(dense_ref, pieces, first, rows):
    total = None
    for at, piece in enumerate(pieces, first):
        depth = piece.shape[0]
        term = jnp.dot(dense_ref[rows, at * depth : (at + 1) * depth], piece[...], preferred_element_type=F32)
        total = term if total is None else total + term
    return total


def forward_early(sent, dense_ref, *refs):
    pieces, total_ref = refs[:-1], refs[-1]
    rows = total_ref.shape[0]
    group = rows // sent
    total_ref[...] = rows_of(dense_ref, pieces, 0, slice(group, group + rows))


def forward_sent(last, dense_ref, total_ref, piece_ref, *outs):
    for m, ref in enumerate(outs):
        group = ref.shape[0]
        total = rows_of(dense_ref, [piece_ref], last, slice((m + 1) * group, (m + 2) * group))
        ref[...] = (total + total_ref[m * group : (m + 1) * group, :]).astype(BF16)


def forward_own(dense_ref, *refs):
    pieces, out_ref = refs[:-1], refs[-1]
    out_ref[...] = rows_of(dense_ref, pieces, 0, slice(0, out_ref.shape[0]))


def project(left_ref, weight_ref, out_ref):
    out_ref[...] = jnp.dot(left_ref[...], weight_ref[...], preferred_element_type=F32)


def middle(near, share, first_ref, left_ref, right_ref, weight_ref, *refs):
    cot_refs, (send_ref, hidden_ref) = refs[:-2], refs[-2:]
    group, width = left_ref.shape
    place = lax.axis_index("col") >> near
    weight = weight_ref[...]
    at = 0
    for cot_ref in cot_refs:
        for start in range(0, cot_ref.shape[0], share):
            rows = pl.ds(pl.multiple_of((place ^ at) * share, share), share)
            summed = first_ref[rows, :] + jnp.dot(right_ref[rows, :], weight, preferred_element_type=F32)
            gate = 1.0 / (1.0 + jnp.exp(-summed))
            if at == 0:
                hidden_ref[...] = (summed * gate).astype(BF16)
            slope = gate * (1.0 + summed * (1.0 - gate))
            send_ref[rows, :] = (cot_ref[start : start + share, :].astype(F32) * slope).astype(BF16)
            at += 1
    both = jnp.concatenate([left_ref[...], right_ref[...]], axis=1)
    term = lax.dot_general(send_ref[:group, :], both, (((0,), (0,)), ((), ())), preferred_element_type=F32)
    send_ref[group:, :] = (term[:, :width] + term[:, width:]).T.astype(BF16)


def emit(given_ref, out_ref):
    out_ref[...] = given_ref[...]


def pair_sums(terms):
    while len(terms) > 1:
        terms = [a + b for a, b in zip(terms[::2], terms[1::2])]
    return terms[0]


def columns_of(dense_ref, grads, first, columns):
    total = None
    for m, grad in enumerate(grads, first):
        group = grad.shape[0] - grad.shape[1]
        term = lax.dot_general(
            grad[:group, :],
            dense_ref[m * group : (m + 1) * group, columns],
            (((0,), (0,)), ((), ())),
            preferred_element_type=F32,
        )
        total = term if total is None else total + term
    return total


def backward_own(dense_ref, grad_ref, total_ref):
    total_ref[...] = columns_of(dense_ref, [grad_ref], 0, slice(0, total_ref.shape[1]))


def backward_sent(dense_ref, total_ref, *refs):
    grads, send_ref = refs[:-1], refs[-1]
    width, kept = total_ref.shape[0], total_ref.shape[1] // 2
    columns = slice(kept, 2 * kept)
    send_ref[:kept, :] = (columns_of(dense_ref, grads[1:], 1, columns) + total_ref[:, columns]).T.astype(BF16)
    term = pair_sums([grad[-width:, :].astype(F32) for grad in grads])
    high = term.astype(BF16)
    send_ref[kept : kept + width, :] = high
    send_ref[kept + width :, :] = (term - high.astype(F32)).astype(BF16)


def backward_kept(dense_ref, total_ref, *refs):
    grads, keep_ref = refs[:-1], refs[-1]
    columns = slice(0, keep_ref.shape[0])
    keep_ref[...] = (columns_of(dense_ref, grads, 1, columns) + total_ref[:, columns]).T


def finish(scale, keep_ref, own_ref, other_ref, weight_ref, grad_ref, wgrad_ref):
    share = keep_ref.shape[0]
    grad_proj = (keep_ref[...] + other_ref[:share, :].astype(F32)).astype(BF16)
    grad_ref[...] = lax.dot_general(
        grad_proj, weight_ref[...], (((1,), (1,)), ((), ())), preferred_element_type=F32
    ).astype(BF16)
    wgrad_ref[...] = (own_ref[share:, :].astype(F32) + other_ref[share:, :].astype(F32)) * scale


def swap(x, axis, mask):
    n = lax.axis_size(axis)
    return lax.ppermute(x, axis, [(i, i ^ mask) for i in range(n)])


class DenseBlock:
    def __init__(self, row_of, col_of, rows, cols, tiles, tile_slots, tile_counts):
        (self.dense,) = kernel_call(
            functools.partial(densify, row_of, col_of, DENSIFY_PARTS),
            [((rows + tiles.shape[-1], cols), BF16, True)],
            0,
            "densify",
            [ANY, ANY, pl.BlockSpec(memory_space=pltpu.SMEM)],
            [
                pltpu.VMEM(tiles.shape[2:], BF16),
                pltpu.SMEM(tile_slots.shape, jnp.int32),
                pltpu.SMEM((rows // tiles.shape[-1],), jnp.int32),
                pltpu.SMEM((cols // tiles.shape[-1],), jnp.int32),
                pltpu.SemaphoreType.DMA((DENSIFY_PARTS + 1,)),
            ],
        )(in_hbm(tiles), in_hbm(tile_slots), tile_counts)
        self.rows, self.cols = rows, cols

    def after(self, x):
        x, self.dense = lax.optimization_barrier((x, self.dense))
        return x

    def forward(self, pieces, groups):
        width, group = pieces[0].shape[-1], self.rows // groups
        sent = groups - 1
        dense = in_vmem(self.dense)
        flops = 2 * group * self.cols * width

        def some(kernel, outs, flops, name, *given):
            return kernel_call(kernel, outs, flops, name, [VM] * (1 + len(given)))(dense, *given)

        last = len(pieces) - 1
        (total,) = some(
            functools.partial(forward_early, sent),
            [((sent * group, width), F32, True)],
            flops * sent * last // len(pieces),
            "forward_early",
            *pieces[:last],
        )
        sends = some(
            functools.partial(forward_sent, last),
            [((group, width), BF16, True)] * sent,
            flops * sent // len(pieces),
            "forward_sent",
            total,
            pieces[last],
        )
        (own,) = some(forward_own, [((group, width), F32, True)], flops, "forward_own", *pieces)
        return [own, *sends]

    def backward(self, grads):
        rows, cols = self.rows, self.cols
        width = grads[0].shape[-1]
        dense = in_vmem(self.dense)

        def some(kernel, shape, dtype, flops, name, *given):
            (out,) = kernel_call(kernel, [(shape, dtype, True)], flops, name, [VM] * (1 + len(given)))(dense, *given)
            return out

        flops = 2 * rows * cols * width // len(grads)
        total = some(backward_own, (width, cols), F32, flops, "backward_own", grads[0])
        flops = 2 * rows * cols * width // 2
        send = some(backward_sent, (cols // 2 + 2 * width, width), BF16, flops, "backward_sent", total, *grads)
        return send, some(backward_kept, (cols // 2, width), F32, flops, "backward_kept", total, *grads[1:])


class TiledBlock:
    def __init__(self, row_of, col_of, rows, cols, tiles, tile_slots, tile_counts):
        self.tiles, slots = tiles[0, 0], tile_slots[0, 0]
        self.size = self.tiles.shape[-1]
        self.row_count, self.col_count = rows // self.size, cols // self.size
        tile_row, tile_col = quotient(slots, self.col_count)
        self.row_at = row_of(tile_row, lax.axis_index("col"))
        self.col_at = col_of(tile_col, lax.axis_index("row"))
        self.live = jnp.arange(slots.shape[0], dtype=jnp.int32) < tile_counts[0, 0]

    def after(self, x):
        return x

    def forward(self, pieces, groups):
        given = jnp.concatenate(pieces).reshape(self.col_count, self.size, -1)[self.col_at]
        terms = jnp.einsum("tij,tjf->tif", self.tiles, given, preferred_element_type=F32)
        at = jnp.where(self.live, self.row_at, self.row_count)
        sums = jax.ops.segment_sum(terms, at, self.row_count + 1)[: self.row_count]
        parts = jnp.split(sums.reshape(-1, given.shape[-1]), groups)
        return [parts[0], *[part.astype(BF16) for part in parts[1:]]]

    def backward(self, grads):
        group = self.row_count * self.size // len(grads)
        given = jnp.concatenate([grad[:group] for grad in grads])
        given = given.reshape(self.row_count, self.size, -1)[self.row_at]
        terms = jnp.einsum("tji,tjf->tif", self.tiles, given, preferred_element_type=F32)
        at = jnp.where(self.live, self.col_at, self.col_count)
        sums = jax.ops.segment_sum(terms, at, self.col_count + 1)[: self.col_count]
        keep, send = jnp.split(sums.reshape(-1, given.shape[-1]), 2)
        wsum = pair_sums([grad[group:].astype(F32) for grad in grads])
        high = lax.reduce_precision(wsum, 8, 7)
        return lax.optimization_barrier(jnp.concatenate([send, high, wsum - high]).astype(BF16)), keep


def body(features, weight, tiles, tile_slots, tile_counts, cotangent):
    size = tiles.shape[-1]
    share, width = features.shape
    row_count, col_count = lax.axis_size("row"), lax.axis_size("col")
    row_bits, col_bits = row_count.bit_length() - 1, col_count.bit_length() - 1
    near = min(2, col_bits)
    rows, cols = share * col_count, share * row_count
    group = rows >> near
    row_of = functools.partial(row_place, near=near, share_tiles=share // size, group_tiles=group // size)
    col_of = functools.partial(col_place, row_bits=row_bits, share_tiles=share // size)
    block_type = DenseBlock if 2 * rows * cols <= DENSE_LIMIT else TiledBlock
    block = block_type(row_of, col_of, rows, cols, tiles, tile_slots, tile_counts)

    pieces = [features]
    for bit in reversed(range(row_bits)):
        pieces += [swap(piece, "row", 1 << bit) for piece in pieces]
        if bit == row_bits - 1:
            pieces[1] = block.after(pieces[1])
    total, *sends = block.forward(pieces, 1 << near)

    sends, cotangent = lax.optimization_barrier((sends, cotangent))
    cots = [cotangent]
    for bit in range(near, col_bits):
        cots += [swap(piece, "col", sum_mask(bit, near)) for piece in cots]

    for send, mask in zip(sends, PARTNERS[near]):
        total = total + swap(send, "col", mask).astype(F32)
    left, cots = lax.optimization_barrier((total.astype(BF16), cots))
    right = jnp.zeros_like(left)
    for bit in range(near, col_bits):
        if bit > near:
            left = lax.optimization_barrier((left.astype(F32) + right.astype(F32)).astype(BF16))
        right = swap(left, "col", sum_mask(bit, near))

    (first,) = kernel_call(
        project, [((group, width), F32, True)], 2 * group * width * width, "project", [VM] * 2
    )(left, weight)
    grads, hidden = kernel_call(
        functools.partial(middle, near, share),
        [((group + width, width), BF16, True), ((share, width), BF16, True)],
        6 * group * width * width,
        "middle",
        [VM] * (4 + len(cots)),
    )(first, left, right, weight, *cots)
    (hidden,) = kernel_call(emit, [((share, width), BF16, False)], 0, "emit", [VM])(hidden)
    send, keep = block.backward([grads, *[swap(grads, "col", mask) for mask in PARTNERS[near]]])

    kept = cols // 2
    for bit in range(row_bits):
        other = swap(send, "row", 1 << bit)
        if bit == row_bits - 1:
            break
        keep = keep + other[:kept].astype(F32)
        terms = [jnp.sum(part[kept:].astype(F32).reshape(-1, width, width), axis=0) for part in (send, other)]
        wsum = pair_sums(terms)
        kept //= 2
        send = lax.optimization_barrier(jnp.concatenate([keep[kept:].astype(BF16), wsum.astype(BF16)]))
        keep = keep[:kept]

    feature_grad, weight_grad = kernel_call(
        functools.partial(finish, 1.0 / math.sqrt(share * row_count * col_count)),
        [((share, width), BF16, False), ((width, width), F32, False)],
        2 * share * width * width,
        "finish",
        [VM] * 4,
    )(keep, send, other, weight)
    return hidden, feature_grad, weight_grad


def solution(mesh):
    placed = (
        P(("col", "row"), None),
        P(),
        P("row", "col", None, None, None),
        P("row", "col", None),
        P("row", "col"),
        P(("row", "col"), None),
    )
    return jax.shard_map(
        body,
        mesh=mesh,
        in_specs=placed,
        out_specs=(P(("row", "col"), None), P(("col", "row"), None), P()),
        check_vma=False,
    )
```

```python
import functools
import math

import jax
import jax.numpy as jnp
from jax import lax
from jax.experimental import pallas as pl
from jax.experimental.pallas import tpu as pltpu
from jax.sharding import PartitionSpec as P

F32 = jnp.float32
BF16 = jnp.bfloat16
VMEM_LIMIT = 24 * 1024 * 1024
DENSIFY_PARTS = 6
DENSE_LIMIT = 12 * 1024 * 1024


def in_vmem(x):
    return pltpu.with_memory_space_constraint(x, pltpu.VMEM)


def in_hbm(x):
    return pltpu.with_memory_space_constraint(x, pltpu.HBM)


def kernel_call(kernel, outs, flops, name, in_specs, scratch=(), limit=VMEM_LIMIT):
    shapes = [pltpu.VMEM(s, d) if keep else jax.ShapeDtypeStruct(s, d) for s, d, keep in outs]
    moved = sum(math.prod(s) * jnp.dtype(d).itemsize for s, d, _ in outs)
    return pl.pallas_call(
        kernel,
        out_shape=shapes,
        in_specs=in_specs,
        out_specs=[pl.BlockSpec(memory_space=pltpu.VMEM)] * len(outs),
        scratch_shapes=list(scratch),
        compiler_params=pltpu.CompilerParams(vmem_limit_bytes=limit),
        cost_estimate=pl.CostEstimate(flops=flops, bytes_accessed=moved, transcendentals=0),
        name=name,
    )


VM = pl.BlockSpec(memory_space=pltpu.VMEM)
ANY = pl.BlockSpec(memory_space=pl.ANY)


def bit_reverse(value, bits):
    out = 0
    for b in range(bits):
        out = out | (((value >> b) & 1) << (bits - 1 - b))
    return out


PARTNERS = {0: [], 1: [1], 2: [2, 1, 3]}


def sum_mask(bit, near):
    return 3 << (bit - 1) if bit == near and near else 1 << bit


def quotient(value, by):
    if by & (by - 1):
        return lax.div(value, by), lax.rem(value, by)
    return value >> (by.bit_length() - 1), value & (by - 1)


def row_place(tile_row, my_col, near, share_tiles, group_tiles):
    share, rest = quotient(tile_row, share_tiles)
    apart = share ^ my_col
    if near:
        apart = apart ^ (((apart >> near) & 1) << (near - 1))
    mask = apart & ((1 << near) - 1)
    group = mask * 0
    for at, partner in enumerate(PARTNERS[near]):
        group = jnp.where(mask == partner, at + 1, group)
    return group * group_tiles + (share >> near) * share_tiles + rest


def col_place(tile_col, my_row, row_bits, share_tiles):
    share, rest = quotient(tile_col, share_tiles)
    return bit_reverse(share ^ my_row, row_bits) * share_tiles + rest


def densify(row_of, col_of, parts, tiles_ref, slots_ref, count_ref, dense_ref, held, slots, row_at, col_at, sems):
    total, size, _ = held.shape
    step = -(-total // parts)
    copies = [pltpu.make_async_copy(slots_ref, slots, sems.at[parts])]
    for part, start in enumerate(range(0, total, step)):
        some = pl.ds(start, min(step, total - start))
        copies.append(pltpu.make_async_copy(tiles_ref.at[0, 0, some], held.at[some], sems.at[part]))
    for copy in copies:
        copy.start()
    dense_ref[...] = jnp.zeros_like(dense_ref)
    my_row, my_col = lax.axis_index("row"), lax.axis_index("col")
    for at in range(row_at.shape[0]):
        row_at[at] = row_of(jnp.int32(at), my_col) * size
    for at in range(col_at.shape[0]):
        col_at[at] = col_of(jnp.int32(at), my_row) * size
    dead = dense_ref.shape[0] - size
    count = count_ref[0, 0]
    copies[0].wait()
    unroll = 4
    for copy, start in zip(copies[1:], range(0, total, step)):
        end = min(start + step, total)
        copy.wait()

        def some_tiles(turn, carry, start=start, end=end):
            for inner in range(unroll):
                k = start + turn * unroll + inner
                at = jnp.minimum(k, end - 1)
                tile_row, tile_col = quotient(slots[0, 0, at], col_at.shape[0])
                row = jnp.where((k < count) & (k < end), row_at[tile_row], dead)
                rows = pl.ds(pl.multiple_of(row, size), size)
                cols = pl.ds(pl.multiple_of(col_at[tile_col], size), size)
                dense_ref[rows, cols] = held[at]
            return carry

        turns = (jnp.clip(count - start, 0, end - start) + unroll - 1) // unroll
        lax.fori_loop(0, turns, some_tiles, 0)


def rows_of(dense_ref, pieces, first, rows):
    total = None
    for at, piece in enumerate(pieces, first):
        depth = piece.shape[0]
        term = jnp.dot(dense_ref[rows, at * depth : (at + 1) * depth], piece[...], preferred_element_type=F32)
        total = term if total is None else total + term
    return total


def forward_early(sent, dense_ref, *refs):
    pieces, total_ref = refs[:-1], refs[-1]
    rows = total_ref.shape[0]
    group = rows // sent
    total_ref[...] = rows_of(dense_ref, pieces, 0, slice(group, group + rows))


def forward_sent(last, dense_ref, total_ref, piece_ref, *outs):
    for m, ref in enumerate(outs):
        group = ref.shape[0]
        total = rows_of(dense_ref, [piece_ref], last, slice((m + 1) * group, (m + 2) * group))
        ref[...] = (total + total_ref[m * group : (m + 1) * group, :]).astype(BF16)


def forward_own(dense_ref, *refs):
    pieces, out_ref = refs[:-1], refs[-1]
    out_ref[...] = rows_of(dense_ref, pieces, 0, slice(0, out_ref.shape[0]))


def project(left_ref, weight_ref, out_ref):
    out_ref[...] = jnp.dot(left_ref[...], weight_ref[...], preferred_element_type=F32)


def middle(near, share, first_ref, left_ref, right_ref, weight_ref, *refs):
    cot_refs, (send_ref, hidden_ref) = refs[:-2], refs[-2:]
    group, width = left_ref.shape
    place = lax.axis_index("col") >> near
    weight = weight_ref[...]
    at = 0
    for cot_ref in cot_refs:
        for start in range(0, cot_ref.shape[0], share):
            rows = pl.ds(pl.multiple_of((place ^ at) * share, share), share)
            summed = first_ref[rows, :] + jnp.dot(right_ref[rows, :], weight, preferred_element_type=F32)
            gate = 1.0 / (1.0 + jnp.exp(-summed))
            if at == 0:
                hidden_ref[...] = (summed * gate).astype(BF16)
            slope = gate * (1.0 + summed * (1.0 - gate))
            send_ref[rows, :] = (cot_ref[start : start + share, :].astype(F32) * slope).astype(BF16)
            at += 1
    both = jnp.concatenate([left_ref[...], right_ref[...]], axis=1)
    term = lax.dot_general(send_ref[:group, :], both, (((0,), (0,)), ((), ())), preferred_element_type=F32)
    send_ref[group:, :] = (term[:, :width] + term[:, width:]).T.astype(BF16)


def emit(given_ref, out_ref):
    out_ref[...] = given_ref[...]


def pair_sums(terms):
    while len(terms) > 1:
        terms = [a + b for a, b in zip(terms[::2], terms[1::2])]
    return terms[0]


def columns_of(dense_ref, grads, first, columns):
    total = None
    for m, grad in enumerate(grads, first):
        group = grad.shape[0] - grad.shape[1]
        term = lax.dot_general(
            grad[:group, :],
            dense_ref[m * group : (m + 1) * group, columns],
            (((0,), (0,)), ((), ())),
            preferred_element_type=F32,
        )
        total = term if total is None else total + term
    return total


def backward_own(dense_ref, grad_ref, total_ref):
    total_ref[...] = columns_of(dense_ref, [grad_ref], 0, slice(0, total_ref.shape[1]))


def backward_sent(dense_ref, total_ref, *refs):
    grads, send_ref = refs[:-1], refs[-1]
    width, kept = total_ref.shape[0], total_ref.shape[1] // 2
    columns = slice(kept, 2 * kept)
    send_ref[:kept, :] = (columns_of(dense_ref, grads[1:], 1, columns) + total_ref[:, columns]).T.astype(BF16)
    term = pair_sums([grad[-width:, :].astype(F32) for grad in grads])
    high = term.astype(BF16)
    send_ref[kept : kept + width, :] = high
    send_ref[kept + width :, :] = (term - high.astype(F32)).astype(BF16)


def backward_kept(dense_ref, total_ref, *refs):
    grads, keep_ref = refs[:-1], refs[-1]
    columns = slice(0, keep_ref.shape[0])
    keep_ref[...] = (columns_of(dense_ref, grads, 1, columns) + total_ref[:, columns]).T


def fold(width, keep_ref, own_ref, other_ref, send_ref, kept_ref):
    whole = keep_ref.shape[0]
    kept = whole // 2
    send_ref[:kept, :] = (keep_ref[kept:, :] + other_ref[kept:whole, :].astype(F32)).astype(BF16)
    terms = []
    for ref in (own_ref, other_ref):
        total = ref[whole : whole + width, :].astype(F32)
        for start in range(whole + width, ref.shape[0], width):
            total += ref[start : start + width, :].astype(F32)
        terms.append(total)
    send_ref[kept:, :] = (terms[0] + terms[1]).astype(BF16)
    kept_ref[...] = keep_ref[:kept, :] + other_ref[:kept, :].astype(F32)


def finish(scale, keep_ref, own_ref, other_ref, weight_ref, grad_ref, wgrad_ref):
    share = keep_ref.shape[0]
    grad_proj = (keep_ref[...] + other_ref[:share, :].astype(F32)).astype(BF16)
    grad_ref[...] = lax.dot_general(
        grad_proj, weight_ref[...], (((1,), (1,)), ((), ())), preferred_element_type=F32
    ).astype(BF16)
    wgrad_ref[...] = (own_ref[share:, :].astype(F32) + other_ref[share:, :].astype(F32)) * scale


def swap(x, axis, mask):
    n = lax.axis_size(axis)
    return lax.ppermute(x, axis, [(i, i ^ mask) for i in range(n)])


class DenseBlock:
    def __init__(self, row_of, col_of, rows, cols, tiles, tile_slots, tile_counts):
        (self.dense,) = kernel_call(
            functools.partial(densify, row_of, col_of, DENSIFY_PARTS),
            [((rows + tiles.shape[-1], cols), BF16, True)],
            0,
            "densify",
            [ANY, ANY, pl.BlockSpec(memory_space=pltpu.SMEM)],
            [
                pltpu.VMEM(tiles.shape[2:], BF16),
                pltpu.SMEM(tile_slots.shape, jnp.int32),
                pltpu.SMEM((rows // tiles.shape[-1],), jnp.int32),
                pltpu.SMEM((cols // tiles.shape[-1],), jnp.int32),
                pltpu.SemaphoreType.DMA((DENSIFY_PARTS + 1,)),
            ],
        )(in_hbm(tiles), in_hbm(tile_slots), tile_counts)
        self.rows, self.cols = rows, cols

    def after(self, x):
        x, self.dense = lax.optimization_barrier((x, self.dense))
        return x

    def forward(self, pieces, groups):
        width, group = pieces[0].shape[-1], self.rows // groups
        sent = groups - 1
        dense = in_vmem(self.dense)
        flops = 2 * group * self.cols * width

        def some(kernel, outs, flops, name, *given):
            return kernel_call(kernel, outs, flops, name, [VM] * (1 + len(given)))(dense, *given)

        last = len(pieces) - 1
        (total,) = some(
            functools.partial(forward_early, sent),
            [((sent * group, width), F32, True)],
            flops * sent * last // len(pieces),
            "forward_early",
            *pieces[:last],
        )
        sends = some(
            functools.partial(forward_sent, last),
            [((group, width), BF16, True)] * sent,
            flops * sent // len(pieces),
            "forward_sent",
            total,
            pieces[last],
        )
        (own,) = some(forward_own, [((group, width), F32, True)], flops, "forward_own", *pieces)
        return [own, *sends]

    def backward(self, grads):
        rows, cols = self.rows, self.cols
        width = grads[0].shape[-1]
        dense = in_vmem(self.dense)

        def some(kernel, shape, dtype, flops, name, *given):
            (out,) = kernel_call(kernel, [(shape, dtype, True)], flops, name, [VM] * (1 + len(given)))(dense, *given)
            return out

        flops = 2 * rows * cols * width // len(grads)
        total = some(backward_own, (width, cols), F32, flops, "backward_own", grads[0])
        flops = 2 * rows * cols * width // 2
        send = some(backward_sent, (cols // 2 + 2 * width, width), BF16, flops, "backward_sent", total, *grads)
        return send, some(backward_kept, (cols // 2, width), F32, flops, "backward_kept", total, *grads[1:])


class TiledBlock:
    def __init__(self, row_of, col_of, rows, cols, tiles, tile_slots, tile_counts):
        self.tiles, slots = tiles[0, 0], tile_slots[0, 0]
        self.size = self.tiles.shape[-1]
        self.row_count, self.col_count = rows // self.size, cols // self.size
        tile_row, tile_col = quotient(slots, self.col_count)
        self.row_at = row_of(tile_row, lax.axis_index("col"))
        self.col_at = col_of(tile_col, lax.axis_index("row"))
        self.live = jnp.arange(slots.shape[0], dtype=jnp.int32) < tile_counts[0, 0]

    def after(self, x):
        return x

    def forward(self, pieces, groups):
        given = jnp.concatenate(pieces).reshape(self.col_count, self.size, -1)[self.col_at]
        terms = jnp.einsum("tij,tjf->tif", self.tiles, given, preferred_element_type=F32)
        at = jnp.where(self.live, self.row_at, self.row_count)
        sums = jax.ops.segment_sum(terms, at, self.row_count + 1)[: self.row_count]
        parts = jnp.split(sums.reshape(-1, given.shape[-1]), groups)
        return [parts[0], *[part.astype(BF16) for part in parts[1:]]]

    def backward(self, grads):
        group = self.row_count * self.size // len(grads)
        given = jnp.concatenate([grad[:group] for grad in grads])
        given = given.reshape(self.row_count, self.size, -1)[self.row_at]
        terms = jnp.einsum("tji,tjf->tif", self.tiles, given, preferred_element_type=F32)
        at = jnp.where(self.live, self.col_at, self.col_count)
        sums = jax.ops.segment_sum(terms, at, self.col_count + 1)[: self.col_count]
        keep, send = jnp.split(sums.reshape(-1, given.shape[-1]), 2)
        wsum = pair_sums([grad[group:].astype(F32) for grad in grads])
        high = lax.reduce_precision(wsum, 8, 7)
        return lax.optimization_barrier(jnp.concatenate([send, high, wsum - high]).astype(BF16)), keep


def body(features, weight, tiles, tile_slots, tile_counts, cotangent):
    size = tiles.shape[-1]
    share, width = features.shape
    row_count, col_count = lax.axis_size("row"), lax.axis_size("col")
    row_bits, col_bits = row_count.bit_length() - 1, col_count.bit_length() - 1
    near = min(2, col_bits)
    rows, cols = share * col_count, share * row_count
    group = rows >> near
    row_of = functools.partial(row_place, near=near, share_tiles=share // size, group_tiles=group // size)
    col_of = functools.partial(col_place, row_bits=row_bits, share_tiles=share // size)
    block_type = DenseBlock if 2 * rows * cols <= DENSE_LIMIT else TiledBlock
    block = block_type(row_of, col_of, rows, cols, tiles, tile_slots, tile_counts)

    pieces = [features]
    for bit in reversed(range(row_bits)):
        pieces += [swap(piece, "row", 1 << bit) for piece in pieces]
        if bit == row_bits - 1:
            pieces[1] = block.after(pieces[1])
    total, *sends = block.forward(pieces, 1 << near)

    sends, cotangent = lax.optimization_barrier((sends, cotangent))
    cots = [cotangent]
    for bit in range(near, col_bits):
        cots += [swap(piece, "col", sum_mask(bit, near)) for piece in cots]

    for send, mask in zip(sends, PARTNERS[near]):
        total = total + swap(send, "col", mask).astype(F32)
    left, cots = lax.optimization_barrier((total.astype(BF16), cots))
    right = jnp.zeros_like(left)
    for bit in range(near, col_bits):
        if bit > near:
            left = lax.optimization_barrier((left.astype(F32) + right.astype(F32)).astype(BF16))
        right = swap(left, "col", sum_mask(bit, near))

    (first,) = kernel_call(
        project, [((group, width), F32, True)], 2 * group * width * width, "project", [VM] * 2
    )(left, weight)
    grads, hidden = kernel_call(
        functools.partial(middle, near, share),
        [((group + width, width), BF16, True), ((share, width), BF16, True)],
        6 * group * width * width,
        "middle",
        [VM] * (4 + len(cots)),
    )(first, left, right, weight, *cots)
    (hidden,) = kernel_call(emit, [((share, width), BF16, False)], 0, "emit", [VM])(hidden)
    send, keep = block.backward([grads, *[swap(grads, "col", mask) for mask in PARTNERS[near]]])

    kept = cols // 2
    for bit in range(row_bits):
        other = swap(send, "row", 1 << bit)
        if bit == row_bits - 1:
            break
        kept //= 2
        send, keep = kernel_call(
            functools.partial(fold, width),
            [((kept + width, width), BF16, True), ((kept, width), F32, True)],
            0,
            "fold",
            [VM] * 3,
        )(keep, send, other)

    feature_grad, weight_grad = kernel_call(
        functools.partial(finish, 1.0 / math.sqrt(share * row_count * col_count)),
        [((share, width), BF16, False), ((width, width), F32, False)],
        2 * share * width * width,
        "finish",
        [VM] * 4,
    )(keep, send, other, weight)
    return hidden, feature_grad, weight_grad


def solution(mesh):
    placed = (
        P(("col", "row"), None),
        P(),
        P("row", "col", None, None, None),
        P("row", "col", None),
        P("row", "col"),
        P(("row", "col"), None),
    )
    return jax.shard_map(
        body,
        mesh=mesh,
        in_specs=placed,
        out_specs=(P(("row", "col"), None), P(("col", "row"), None), P()),
        check_vma=False,
    )
```

```python
import functools
import math

import jax
import jax.numpy as jnp
from jax import lax
from jax.experimental import pallas as pl
from jax.experimental.pallas import tpu as pltpu
from jax.sharding import PartitionSpec as P

F32 = jnp.float32
BF16 = jnp.bfloat16
VMEM_LIMIT = 24 * 1024 * 1024
DENSIFY_PARTS = 6
DENSE_LIMIT = 12 * 1024 * 1024


def in_vmem(x):
    return pltpu.with_memory_space_constraint(x, pltpu.VMEM)


def in_hbm(x):
    return pltpu.with_memory_space_constraint(x, pltpu.HBM)


def kernel_call(kernel, outs, flops, name, in_specs, scratch=(), limit=VMEM_LIMIT):
    shapes = [pltpu.VMEM(s, d) if keep else jax.ShapeDtypeStruct(s, d) for s, d, keep in outs]
    moved = sum(math.prod(s) * jnp.dtype(d).itemsize for s, d, _ in outs)
    return pl.pallas_call(
        kernel,
        out_shape=shapes,
        in_specs=in_specs,
        out_specs=[pl.BlockSpec(memory_space=pltpu.VMEM)] * len(outs),
        scratch_shapes=list(scratch),
        compiler_params=pltpu.CompilerParams(vmem_limit_bytes=limit),
        cost_estimate=pl.CostEstimate(flops=flops, bytes_accessed=moved, transcendentals=0),
        name=name,
    )


VM = pl.BlockSpec(memory_space=pltpu.VMEM)
ANY = pl.BlockSpec(memory_space=pl.ANY)


def bit_reverse(value, bits):
    out = 0
    for b in range(bits):
        out = out | (((value >> b) & 1) << (bits - 1 - b))
    return out


PARTNERS = {0: [], 1: [1], 2: [2, 1, 3]}


def sum_mask(bit, near):
    return 3 << (bit - 1) if bit == near and near else 1 << bit


def quotient(value, by):
    if by & (by - 1):
        return lax.div(value, by), lax.rem(value, by)
    return value >> (by.bit_length() - 1), value & (by - 1)


def row_place(tile_row, my_col, near, share_tiles, group_tiles):
    share, rest = quotient(tile_row, share_tiles)
    apart = share ^ my_col
    if near:
        apart = apart ^ (((apart >> near) & 1) << (near - 1))
    mask = apart & ((1 << near) - 1)
    group = mask * 0
    for at, partner in enumerate(PARTNERS[near]):
        group = jnp.where(mask == partner, at + 1, group)
    return group * group_tiles + (share >> near) * share_tiles + rest


def col_place(tile_col, my_row, row_bits, share_tiles):
    share, rest = quotient(tile_col, share_tiles)
    return bit_reverse(share ^ my_row, row_bits) * share_tiles + rest


def densify(row_of, col_of, parts, tiles_ref, slots_ref, count_ref, dense_ref, held, slots, row_at, col_at, sems):
    total, size, _ = held.shape
    step = -(-total // parts)
    copies = [pltpu.make_async_copy(slots_ref, slots, sems.at[parts])]
    for part, start in enumerate(range(0, total, step)):
        some = pl.ds(start, min(step, total - start))
        copies.append(pltpu.make_async_copy(tiles_ref.at[0, 0, some], held.at[some], sems.at[part]))
    for copy in copies:
        copy.start()
    dense_ref[...] = jnp.zeros_like(dense_ref)
    my_row, my_col = lax.axis_index("row"), lax.axis_index("col")
    for at in range(row_at.shape[0]):
        row_at[at] = row_of(jnp.int32(at), my_col) * size
    for at in range(col_at.shape[0]):
        col_at[at] = col_of(jnp.int32(at), my_row) * size
    dead = dense_ref.shape[0] - size
    count = count_ref[0, 0]
    copies[0].wait()
    unroll = 4
    for copy, start in zip(copies[1:], range(0, total, step)):
        end = min(start + step, total)
        copy.wait()

        def some_tiles(turn, carry, start=start, end=end):
            for inner in range(unroll):
                k = start + turn * unroll + inner
                at = jnp.minimum(k, end - 1)
                tile_row, tile_col = quotient(slots[0, 0, at], col_at.shape[0])
                row = jnp.where((k < count) & (k < end), row_at[tile_row], dead)
                rows = pl.ds(pl.multiple_of(row, size), size)
                cols = pl.ds(pl.multiple_of(col_at[tile_col], size), size)
                dense_ref[rows, cols] = held[at]
            return carry

        turns = (jnp.clip(count - start, 0, end - start) + unroll - 1) // unroll
        lax.fori_loop(0, turns, some_tiles, 0)


def rows_of(dense_ref, pieces, first, rows):
    total = None
    for at, piece in enumerate(pieces, first):
        depth = piece.shape[0]
        term = jnp.dot(dense_ref[rows, at * depth : (at + 1) * depth], piece[...], preferred_element_type=F32)
        total = term if total is None else total + term
    return total


def forward_early(sent, dense_ref, *refs):
    pieces, total_ref = refs[:-1], refs[-1]
    rows = total_ref.shape[0]
    group = rows // sent
    total_ref[...] = rows_of(dense_ref, pieces, 0, slice(group, group + rows))


def forward_sent(last, dense_ref, total_ref, piece_ref, *outs):
    for m, ref in enumerate(outs):
        group = ref.shape[0]
        total = rows_of(dense_ref, [piece_ref], last, slice((m + 1) * group, (m + 2) * group))
        ref[...] = (total + total_ref[m * group : (m + 1) * group, :]).astype(BF16)


def forward_own(dense_ref, *refs):
    pieces, out_ref = refs[:-1], refs[-1]
    out_ref[...] = rows_of(dense_ref, pieces, 0, slice(0, out_ref.shape[0]))


def project(left_ref, weight_ref, out_ref):
    out_ref[...] = jnp.dot(left_ref[...], weight_ref[...], preferred_element_type=F32)


def middle(near, share, first_ref, left_ref, right_ref, weight_ref, *refs):
    cot_refs, (send_ref, hidden_ref) = refs[:-2], refs[-2:]
    group, width = left_ref.shape
    place = lax.axis_index("col") >> near
    weight = weight_ref[...]
    at = 0
    for cot_ref in cot_refs:
        for start in range(0, cot_ref.shape[0], share):
            rows = pl.ds(pl.multiple_of((place ^ at) * share, share), share)
            summed = first_ref[rows, :] + jnp.dot(right_ref[rows, :], weight, preferred_element_type=F32)
            gate = 1.0 / (1.0 + jnp.exp(-summed))
            if at == 0:
                hidden_ref[...] = (summed * gate).astype(BF16)
            slope = gate * (1.0 + summed * (1.0 - gate))
            send_ref[rows, :] = (cot_ref[start : start + share, :].astype(F32) * slope).astype(BF16)
            at += 1
    both = jnp.concatenate([left_ref[...], right_ref[...]], axis=1)
    term = lax.dot_general(send_ref[:group, :], both, (((0,), (0,)), ((), ())), preferred_element_type=F32)
    send_ref[group:, :] = (term[:, :width] + term[:, width:]).T.astype(BF16)


def emit(given_ref, out_ref):
    out_ref[...] = given_ref[...]


def pair_sums(terms):
    while len(terms) > 1:
        terms = [a + b for a, b in zip(terms[::2], terms[1::2])]
    return terms[0]


def columns_of(dense_ref, grads, first, columns):
    total = None
    for m, grad in enumerate(grads, first):
        group = grad.shape[0] - grad.shape[1]
        term = lax.dot_general(
            grad[:group, :],
            dense_ref[m * group : (m + 1) * group, columns],
            (((0,), (0,)), ((), ())),
            preferred_element_type=F32,
        )
        total = term if total is None else total + term
    return total


def backward_own(dense_ref, grad_ref, total_ref):
    total_ref[...] = columns_of(dense_ref, [grad_ref], 0, slice(0, total_ref.shape[1]))


def backward_more(group, dense_ref, grad_ref, before_ref, total_ref):
    total_ref[...] = columns_of(dense_ref, [grad_ref], group, slice(0, total_ref.shape[1])) + before_ref[...]


def backward_sent(dense_ref, total_ref, *refs):
    grads, send_ref = refs[:-1], refs[-1]
    width, kept = total_ref.shape[0], total_ref.shape[1] // 2
    columns = slice(kept, 2 * kept)
    send_ref[:kept, :] = (columns_of(dense_ref, grads[1:2], 1, columns) + total_ref[:, columns]).T.astype(BF16)
    term = pair_sums([grad[-width:, :].astype(F32) for grad in grads])
    high = term.astype(BF16)
    send_ref[kept : kept + width, :] = high
    send_ref[kept + width :, :] = (term - high.astype(F32)).astype(BF16)


def backward_kept(dense_ref, total_ref, *refs):
    grads, keep_ref = refs[:-1], refs[-1]
    columns = slice(0, keep_ref.shape[0])
    keep_ref[...] = (columns_of(dense_ref, grads, 1, columns) + total_ref[:, columns]).T


def fold(width, keep_ref, own_ref, other_ref, send_ref, kept_ref):
    whole = keep_ref.shape[0]
    kept = whole // 2
    send_ref[:kept, :] = (keep_ref[kept:, :] + other_ref[kept:whole, :].astype(F32)).astype(BF16)
    terms = []
    for ref in (own_ref, other_ref):
        total = ref[whole : whole + width, :].astype(F32)
        for start in range(whole + width, ref.shape[0], width):
            total += ref[start : start + width, :].astype(F32)
        terms.append(total)
    send_ref[kept:, :] = (terms[0] + terms[1]).astype(BF16)
    kept_ref[...] = keep_ref[:kept, :] + other_ref[:kept, :].astype(F32)


def finish(scale, keep_ref, own_ref, other_ref, weight_ref, grad_ref, wgrad_ref):
    share = keep_ref.shape[0]
    grad_proj = (keep_ref[...] + other_ref[:share, :].astype(F32)).astype(BF16)
    grad_ref[...] = lax.dot_general(
        grad_proj, weight_ref[...], (((1,), (1,)), ((), ())), preferred_element_type=F32
    ).astype(BF16)
    wgrad_ref[...] = (own_ref[share:, :].astype(F32) + other_ref[share:, :].astype(F32)) * scale


def swap(x, axis, mask):
    n = lax.axis_size(axis)
    return lax.ppermute(x, axis, [(i, i ^ mask) for i in range(n)])


class DenseBlock:
    def __init__(self, row_of, col_of, rows, cols, tiles, tile_slots, tile_counts):
        (self.dense,) = kernel_call(
            functools.partial(densify, row_of, col_of, DENSIFY_PARTS),
            [((rows + tiles.shape[-1], cols), BF16, True)],
            0,
            "densify",
            [ANY, ANY, pl.BlockSpec(memory_space=pltpu.SMEM)],
            [
                pltpu.VMEM(tiles.shape[2:], BF16),
                pltpu.SMEM(tile_slots.shape, jnp.int32),
                pltpu.SMEM((rows // tiles.shape[-1],), jnp.int32),
                pltpu.SMEM((cols // tiles.shape[-1],), jnp.int32),
                pltpu.SemaphoreType.DMA((DENSIFY_PARTS + 1,)),
            ],
        )(in_hbm(tiles), in_hbm(tile_slots), tile_counts)
        self.rows, self.cols = rows, cols

    def after(self, x):
        x, self.dense = lax.optimization_barrier((x, self.dense))
        return x

    def forward(self, pieces, groups):
        width, group = pieces[0].shape[-1], self.rows // groups
        sent = groups - 1
        dense = in_vmem(self.dense)
        flops = 2 * group * self.cols * width

        def some(kernel, outs, flops, name, *given):
            return kernel_call(kernel, outs, flops, name, [VM] * (1 + len(given)))(dense, *given)

        last = len(pieces) - 1
        (total,) = some(
            functools.partial(forward_early, sent),
            [((sent * group, width), F32, True)],
            flops * sent * last // len(pieces),
            "forward_early",
            *pieces[:last],
        )
        sends = some(
            functools.partial(forward_sent, last),
            [((group, width), BF16, True)] * sent,
            flops * sent // len(pieces),
            "forward_sent",
            total,
            pieces[last],
        )
        (own,) = some(forward_own, [((group, width), F32, True)], flops, "forward_own", *pieces)
        return [own, *sends]

    def backward(self, grads):
        rows, cols = self.rows, self.cols
        width = grads[0].shape[-1]
        dense = in_vmem(self.dense)

        def some(kernel, shape, dtype, flops, name, *given):
            (out,) = kernel_call(kernel, [(shape, dtype, True)], flops, name, [VM] * (1 + len(given)))(dense, *given)
            return out

        flops = 2 * rows * cols * width // len(grads)
        total = some(backward_own, (width, cols), F32, flops, "backward_own", grads[0])
        for m in range(len(grads) - 1, 1, -1):
            more = functools.partial(backward_more, m)
            total = some(more, (width, cols), F32, flops, "backward_more", grads[m], total)
        flops = 2 * rows * cols * width // 2
        send = some(backward_sent, (cols // 2 + 2 * width, width), BF16, flops, "backward_sent", total, *grads)
        return send, some(backward_kept, (cols // 2, width), F32, flops, "backward_kept", total, *grads[1:2])


class TiledBlock:
    def __init__(self, row_of, col_of, rows, cols, tiles, tile_slots, tile_counts):
        self.tiles, slots = tiles[0, 0], tile_slots[0, 0]
        self.size = self.tiles.shape[-1]
        self.row_count, self.col_count = rows // self.size, cols // self.size
        tile_row, tile_col = quotient(slots, self.col_count)
        self.row_at = row_of(tile_row, lax.axis_index("col"))
        self.col_at = col_of(tile_col, lax.axis_index("row"))
        self.live = jnp.arange(slots.shape[0], dtype=jnp.int32) < tile_counts[0, 0]

    def after(self, x):
        return x

    def forward(self, pieces, groups):
        given = jnp.concatenate(pieces).reshape(self.col_count, self.size, -1)[self.col_at]
        terms = jnp.einsum("tij,tjf->tif", self.tiles, given, preferred_element_type=F32)
        at = jnp.where(self.live, self.row_at, self.row_count)
        sums = jax.ops.segment_sum(terms, at, self.row_count + 1)[: self.row_count]
        parts = jnp.split(sums.reshape(-1, given.shape[-1]), groups)
        return [parts[0], *[part.astype(BF16) for part in parts[1:]]]

    def backward(self, grads):
        group = self.row_count * self.size // len(grads)
        given = jnp.concatenate([grad[:group] for grad in grads])
        given = given.reshape(self.row_count, self.size, -1)[self.row_at]
        terms = jnp.einsum("tji,tjf->tif", self.tiles, given, preferred_element_type=F32)
        at = jnp.where(self.live, self.col_at, self.col_count)
        sums = jax.ops.segment_sum(terms, at, self.col_count + 1)[: self.col_count]
        keep, send = jnp.split(sums.reshape(-1, given.shape[-1]), 2)
        wsum = pair_sums([grad[group:].astype(F32) for grad in grads])
        high = lax.reduce_precision(wsum, 8, 7)
        return lax.optimization_barrier(jnp.concatenate([send, high, wsum - high]).astype(BF16)), keep


def body(features, weight, tiles, tile_slots, tile_counts, cotangent):
    size = tiles.shape[-1]
    share, width = features.shape
    row_count, col_count = lax.axis_size("row"), lax.axis_size("col")
    row_bits, col_bits = row_count.bit_length() - 1, col_count.bit_length() - 1
    near = min(2, col_bits)
    rows, cols = share * col_count, share * row_count
    group = rows >> near
    row_of = functools.partial(row_place, near=near, share_tiles=share // size, group_tiles=group // size)
    col_of = functools.partial(col_place, row_bits=row_bits, share_tiles=share // size)
    block_type = DenseBlock if 2 * rows * cols <= DENSE_LIMIT else TiledBlock
    block = block_type(row_of, col_of, rows, cols, tiles, tile_slots, tile_counts)

    pieces = [features]
    for bit in reversed(range(row_bits)):
        pieces += [swap(piece, "row", 1 << bit) for piece in pieces]
        if bit == row_bits - 1:
            pieces[1] = block.after(pieces[1])
    total, *sends = block.forward(pieces, 1 << near)

    sends, cotangent = lax.optimization_barrier((sends, cotangent))
    cots = [cotangent]
    for bit in range(near, col_bits):
        cots += [swap(piece, "col", sum_mask(bit, near)) for piece in cots]

    for send, mask in zip(sends, PARTNERS[near]):
        total = total + swap(send, "col", mask).astype(F32)
    left, cots = lax.optimization_barrier((total.astype(BF16), cots))
    right = jnp.zeros_like(left)
    for bit in range(near, col_bits):
        if bit > near:
            left = lax.optimization_barrier((left.astype(F32) + right.astype(F32)).astype(BF16))
        right = swap(left, "col", sum_mask(bit, near))

    (first,) = kernel_call(
        project, [((group, width), F32, True)], 2 * group * width * width, "project", [VM] * 2
    )(left, weight)
    grads, hidden = kernel_call(
        functools.partial(middle, near, share),
        [((group + width, width), BF16, True), ((share, width), BF16, True)],
        6 * group * width * width,
        "middle",
        [VM] * (4 + len(cots)),
    )(first, left, right, weight, *cots)
    (hidden,) = kernel_call(emit, [((share, width), BF16, False)], 0, "emit", [VM])(hidden)
    send, keep = block.backward([grads, *[swap(grads, "col", mask) for mask in PARTNERS[near]]])

    kept = cols // 2
    for bit in range(row_bits):
        other = swap(send, "row", 1 << bit)
        if bit == row_bits - 1:
            break
        kept //= 2
        send, keep = kernel_call(
            functools.partial(fold, width),
            [((kept + width, width), BF16, True), ((kept, width), F32, True)],
            0,
            "fold",
            [VM] * 3,
        )(keep, send, other)

    feature_grad, weight_grad = kernel_call(
        functools.partial(finish, 1.0 / math.sqrt(share * row_count * col_count)),
        [((share, width), BF16, False), ((width, width), F32, False)],
        2 * share * width * width,
        "finish",
        [VM] * 4,
    )(keep, send, other, weight)
    return hidden, feature_grad, weight_grad


def solution(mesh):
    placed = (
        P(("col", "row"), None),
        P(),
        P("row", "col", None, None, None),
        P("row", "col", None),
        P("row", "col"),
        P(("row", "col"), None),
    )
    return jax.shard_map(
        body,
        mesh=mesh,
        in_specs=placed,
        out_specs=(P(("row", "col"), None), P(("col", "row"), None), P()),
        check_vma=False,
    )
```
